512 devices in a mesh: cfg: 2 (over y_lo), patch: 64 (over z, x, core), rep: 4 (over y_hi).
Axes of the slice: x: 4, y: 8 (y_hi: 4, y_lo: 2; y = y_hi * 2 + y_lo), z: 8, core: 2. Of those that a mesh axis runs over, the one named last changes fastest.
Arguments:
- queries: bfloat16 [2, 2560, 6144], P('cfg', 'patch', 'rep'), parts along dimension 2, may hold values from -8 to 8
- fresh_keys: bfloat16 [2, 2560, 6144], P('cfg', 'patch', 'rep'), parts along dimension 2, may hold values from -8 to 8
- fresh_values: bfloat16 [2, 2560, 6144], P('cfg', 'patch', 'rep'), parts along dimension 2, may hold values from -6 to 6
- stale_keys: bfloat16 [2, 2560, 6144], P('cfg', 'patch', 'rep'), parts along dimension 2, may hold values from -6 to 6
- stale_values: bfloat16 [2, 2560, 6144], P('cfg', 'patch', 'rep'), parts along dimension 2, may hold values from -6 to 6
- text_keys: bfloat16 [2, 1024, 1536], P('cfg', 'rep'), parts along dimension 1, may hold values from -8 to 8
- text_values: bfloat16 [2, 1024, 1536], P('cfg', 'rep'), parts along dimension 1, may hold values from -6 to 6
- text_count: int32 [2], P('cfg'), may hold values from 64 to 256, as said below
- positions: int32 [12, 2560], P('rep', 'patch'), parts along dimension 0, may hold values from 0 to 15, as said below
- mod_shift: float32 [2, 1536], P('cfg'), may hold values from -3 to 3
- mod_scale: float32 [2, 1536], P('cfg'), may hold values from -1.5 to 1.5
- proj_out: bfloat16 [1536, 64], replicated, may hold values from -0.15625 to 0.15625
Outputs:
- guided: float32 [2, 2560, 128], P('cfg', 'patch', 'rep'), parts along dimension 2
The draws below stay inside these ranges and needn't reach their ends.
There are 4 independent parts, one for each index of `rep`. The reference program is written for one: setup_inputs(seed, part) draws one part's arguments, and reference() takes and returns one part's arrays. A program takes and returns all parts, laid end to end along the dimension named above; an argument that names none is the same for every part. Nothing has to cross between parts.
Inputs may be any that keep to these rules, and one draw needn't show every extreme that they name: `positions`: each token has its own cell in a video of 16 x 16 cells a frame, numbered in raster order; the 40 tokens of one device are consecutive cells. `text_count`: one of the two branches has all 256 text tokens live, the other fewer.
All inputs are finite; a program needn't handle non-finite values.
Results may differ from the reference program's by a relative error of at most 0.009.
Values may be sent and summed in bfloat16 or wider, within the bound.
A program may use at most 128 MiB of HBM per device.

```python
import math
import jax
import jax.numpy as jnp
from jax import lax

HEADS = 12
HEAD_DIM = 128
TEXT_LEN = 256
LATENT_CH = 64
TOK_DEV = 40
TOKENS = 2560
FEATURES = 1536


def shared_positions(key):
    order = jax.random.permutation(jax.random.fold_in(key, 101), TOKENS // TOK_DEV)
    flat = (order[:, None] * TOK_DEV + jnp.arange(TOK_DEV)[None, :]).reshape(TOKENS)
    return jnp.stack([flat // 256, flat // 16 % 16, flat % 16]).astype(jnp.int32)


def draw_positions(key, part):
    return shared_positions(key)


def draw_text_count(key, part):
    key = jax.random.fold_in(key, 5)
    first_key, second_key = jax.random.split(key)
    partial_count = jax.random.randint(first_key, (), TEXT_LEN // 4, TEXT_LEN)
    full_branch = jax.random.randint(second_key, (), 0, 2)
    return jnp.where(jnp.arange(2) == full_branch, TEXT_LEN, partial_count).astype(jnp.int32)


def draw_queries(key, part):
    key = jax.random.fold_in(key, 2)
    shaped = (2, TOKENS, HEADS * HEAD_DIM)
    base = jnp.clip(jax.random.normal(key, shaped, jnp.float32), -6.0, 6.0)
    return base.astype(jnp.bfloat16)


def draw_fresh_keys(key, part):
    key = jax.random.fold_in(key, 1)
    shaped = (2, TOKENS, HEADS * HEAD_DIM)
    base = jnp.clip(jax.random.normal(key, shaped, jnp.float32), -6.0, 6.0)
    return base.astype(jnp.bfloat16)


def draw_text_keys(key, part):
    key = jax.random.fold_in(key, 3)
    shaped = (2, TEXT_LEN, HEADS * HEAD_DIM)
    base = jnp.clip(jax.random.normal(key, shaped, jnp.float32), -6.0, 6.0)
    return base.astype(jnp.bfloat16)


def steps_of(rng, dims, cuts, low, top_value):
    level, own = 1.0, jax.random.fold_in(rng, 6)
    for axis_at, parts in cuts:
        steps = jnp.exp(jax.random.uniform(jax.random.fold_in(own, axis_at), (parts,), jnp.float32, low / len(cuts), top_value / len(cuts)))
        level = level * jnp.repeat(steps, dims[axis_at] // parts).reshape([-1 if axis == axis_at else 1 for axis in range(len(dims))])
    return level


def scatter_about(stream_key, shape, width, limit, cuts=(), held_as=jnp.bfloat16):
    values = width * jax.random.normal(stream_key, shape, jnp.float32)
    if cuts:
        values = values * steps_of(stream_key, shape, cuts, -0.22, 0.18)
    return jnp.clip(values, -limit, limit).astype(held_as)


def setup_inputs(seed: int = 0, part: int = 0) -> dict:
    key_list = jax.random.split(jax.random.key(seed), 13)
    part_keys = jax.random.split(jax.random.fold_in(key_list[12], part), 13)
    return {
        "queries": draw_queries(jax.random.fold_in(jax.random.fold_in(key_list[12], part), 71), part),
        "fresh_keys": draw_fresh_keys(jax.random.fold_in(jax.random.fold_in(key_list[12], part), 71), part),
        "fresh_values": scatter_about(part_keys[2], (2, TOKENS, FEATURES), 1.0, 6.0, ((0, 2), (1, 64))),
        "stale_keys": scatter_about(part_keys[3], (2, TOKENS, FEATURES), 1.0, 6.0, ((0, 2), (1, 64))),
        "stale_values": scatter_about(part_keys[4], (2, TOKENS, FEATURES), 1.0, 6.0, ((0, 2), (1, 64))),
        "text_keys": draw_text_keys(jax.random.fold_in(jax.random.fold_in(key_list[12], part), 71), part),
        "text_values": scatter_about(part_keys[6], (2, TEXT_LEN, FEATURES), 1.0, 6.0, ((0, 2),)),
        "text_count": draw_text_count(jax.random.fold_in(key_list[12], 71), part),
        "positions": draw_positions(jax.random.fold_in(jax.random.fold_in(key_list[12], part), 71), part),
        "mod_shift": scatter_about(key_list[9], (2, FEATURES), 0.5, 3.0, ((0, 2),), jnp.float32),
        "mod_scale": scatter_about(key_list[10], (2, FEATURES), 0.3, 1.5, ((0, 2),), jnp.float32),
        "proj_out": scatter_about(key_list[11], (FEATURES, LATENT_CH), FEATURES ** -0.5, 0.15625),
    }


GUIDANCE = 4.0
EPSILON = 1e-06

def rope_angles(positions, head_dim):
    time_extent = head_dim // 8
    space_extent = (head_dim - time_extent) // 2
    pieces = []
    for axis_number, extent in ((0, time_extent), (1, space_extent), (2, space_extent)):
        frequency = 256.0 ** (-jnp.arange(0, extent, 2).astype(jnp.float32) / extent)
        pieces.append(positions[axis_number].astype(jnp.float32)[:, None] * frequency[None, :])
    return jnp.concatenate(pieces, axis=1)

def rotate(values, angles):
    pairs = values.reshape(values.shape[0], values.shape[1], values.shape[2] // 2, 2)
    cosine = jnp.cos(angles)[:, None, :]
    sine_part = jnp.sin(angles)[:, None, :]
    first = pairs[..., 0]
    second = pairs[..., 1]
    turned = jnp.stack([first * cosine - second * sine_part, first * sine_part + second * cosine], axis=-1)
    return turned.reshape(values.shape)

def reference(queries, fresh_keys, fresh_values, stale_keys, stale_values, text_keys, text_values, text_count, positions, mod_shift, mod_scale, proj_out):
    angles = rope_angles(positions, HEAD_DIM)
    factor = 1.0 / math.sqrt(HEAD_DIM)
    blocks = jnp.arange(TOKENS) // TOK_DEV
    same_block = blocks[:, None] == blocks[None, :]
    predictions = []
    for branch in range(2):

        def split_heads(array):
            return array[branch].reshape(array.shape[1], HEADS, HEAD_DIM)
        rot_queries = rotate(split_heads(queries).astype(jnp.float32), angles).astype(jnp.bfloat16)
        rot_keys = rotate(split_heads(fresh_keys).astype(jnp.float32), angles).astype(jnp.bfloat16)
        text_live = jnp.arange(TEXT_LEN) < text_count[branch]

        def per_head(operands):
            query_h, key_h, value_h, stale_kh, stale_vh, word_kh, word_vh = operands
            fresh_scores = jnp.dot(query_h, key_h.T, preferred_element_type=jnp.float32) * factor
            stale_scores = jnp.dot(query_h, stale_kh.T, preferred_element_type=jnp.float32) * factor
            pair_scores = jnp.where(same_block, fresh_scores, stale_scores)
            word_scores = jnp.where(text_live[None, :], jnp.dot(query_h, word_kh.T, preferred_element_type=jnp.float32) * factor, -jnp.inf)
            highest = jnp.maximum(lax.optimization_barrier(jnp.max(pair_scores, axis=1)), lax.optimization_barrier(jnp.max(word_scores, axis=1)))
            pair_weights = jnp.exp(pair_scores - highest[:, None])
            word_weights = jnp.exp(word_scores - highest[:, None])
            totals = lax.optimization_barrier(jnp.sum(pair_weights, axis=1)) + lax.optimization_barrier(jnp.sum(word_weights, axis=1))
            pair_rounded = pair_weights.astype(jnp.bfloat16)
            word_rounded = word_weights.astype(jnp.bfloat16)
            nothing = jnp.zeros((), jnp.bfloat16)
            summed = jnp.dot(jnp.where(same_block, pair_rounded, nothing), value_h, preferred_element_type=jnp.float32)
            summed = summed + jnp.dot(jnp.where(same_block, nothing, pair_rounded), stale_vh, preferred_element_type=jnp.float32)
            summed = summed + jnp.dot(word_rounded, word_vh, preferred_element_type=jnp.float32)
            return summed / totals[:, None]
        stacked = tuple((jnp.swapaxes(array, 0, 1) for array in (rot_queries, rot_keys, split_heads(fresh_values), split_heads(stale_keys), split_heads(stale_values), split_heads(text_keys), split_heads(text_values))))
        attended = lax.map(per_head, stacked)
        attended = jnp.swapaxes(attended, 0, 1).reshape(TOKENS, HEADS * HEAD_DIM)
        center = attended - lax.optimization_barrier(jnp.mean(attended, axis=1, keepdims=True))
        normed = center * lax.rsqrt(lax.optimization_barrier(jnp.mean(center * center, axis=1, keepdims=True)) + EPSILON)
        modulated = (normed * (1.0 + mod_scale[branch]) + mod_shift[branch]).astype(jnp.bfloat16)
        predictions.append(jnp.dot(modulated, proj_out, preferred_element_type=jnp.float32))
    guided = (1.0 - GUIDANCE) * predictions[0] + GUIDANCE * predictions[1]
    return jnp.swapaxes(guided.reshape(TOKENS, 2, LATENT_CH // 2), 0, 1)
```

```python
import math

import jax
import jax.numpy as jnp
import numpy as np
from jax import lax
from jax.experimental import pallas as pl
from jax.experimental.pallas import tpu as pltpu
from jax.sharding import PartitionSpec as P

HEADS = 12
HEAD_DIM = 128
GUIDANCE = 4.0
EPSILON = 1e-06

NX = 4
NC = 2
GROUP_HEADS = HEADS // NX
GW = GROUP_HEADS * HEAD_DIM
SCALE2 = math.log2(math.e) / math.sqrt(HEAD_DIM)
F32 = jnp.float32
BF16 = jnp.bfloat16
MESH = pl.DeviceIdType.MESH


def lane_frequencies():
    time_extent = HEAD_DIM // 8
    space_extent = (HEAD_DIM - time_extent) // 2
    rows = np.zeros((3, HEAD_DIM), np.float32)
    start = 0
    for axis, extent in enumerate((time_extent, space_extent, space_extent)):
        exponent = -np.arange(0, extent, 2).astype(np.float32) / np.float32(extent)
        frequency = (256.0 ** exponent.astype(np.float64)).astype(np.float32)
        rows[axis, start : start + extent] = np.repeat(frequency, 2)
        start += extent
    return rows


def copy_keys(nz):
    half = nz // 2
    keys = [("in", name, d) for name in ("sk", "sv", "q", "fk", "fv") for d in range(1, NX)]
    for kv in ("k", "v"):
        for d in range(NX):
            keys += [("z", kv, 1, d), ("z", kv, nz - 1, d), ("s", kv, 0, d)]
        for r in range(1, nz):
            keys.append(("s", kv, r))
            if r not in (1, nz - 1):
                keys.append(("z", kv, r))
    keys += [("o", d) for d in range(1, NX)]
    keys.append(("cfg",))
    return keys


def kernel(
    nz,
    rows,
    q_hbm,
    fk_hbm,
    fv_hbm,
    sk_hbm,
    sv_hbm,
    tk_hbm,
    tv_hbm,
    shift_hbm,
    scale_hbm,
    proj_hbm,
    cnt_ref,
    pos_ref,
    freq_ref,
    out_ref,
    raw,
    qsend,
    fksend,
    qbuf,
    fkbuf,
    fvbuf,
    kbuf,
    vbuf,
    tkbuf,
    tvbuf,
    shiftbuf,
    scalebuf,
    projbuf,
    qh,
    top,
    total,
    acc,
    osend,
    orecv,
    psend,
    precv,
    local_sem,
    send_sem,
    recv_sem,
):
    keys = {key: i for i, key in enumerate(copy_keys(nz))}
    half = nz // 2
    patch = lax.axis_index("patch")
    branch = lax.axis_index("cfg")
    core = lax.rem(patch, NC)
    x = lax.rem(patch // NC, NX)
    z = patch // (NC * NX)

    def at(zz, xx, cc):
        return {"patch": (zz * NX + xx) * NC + cc}

    def owner(d):
        return lax.rem(x + NX - d, NX)

    def asker(d):
        return lax.rem(x + d, NX)

    up = at(lax.rem(z + 1, nz), x, core)
    down = at(lax.rem(z + nz - 1, nz), x, core)
    sibling = at(z, x, 1 - core)
    partner = {"cfg": 1 - branch}

    started = {}

    def send(key, src, dst, device):
        i = keys[key]
        copy = pltpu.make_async_remote_copy(
            src_ref=src,
            dst_ref=dst,
            send_sem=send_sem.at[i],
            recv_sem=recv_sem.at[i],
            device_id=device,
            device_id_type=MESH,
        )
        copy.start()
        started[key] = copy

    def arrived(key):
        started[key].wait_recv()

    locals_ = {}

    def fetch(name, src, dst):
        copy = pltpu.make_async_copy(src, dst, local_sem.at[len(locals_)])
        copy.start()
        locals_[name] = copy

    def columns(group):
        return pl.ds(pl.multiple_of(group * GW, 128), GW)

    fetch("sk", sk_hbm.at[0, :, columns(x)], kbuf.at[0, 0, 0])
    fetch("sv", sv_hbm.at[0, :, columns(x)], vbuf.at[0, 0, 0])
    fetch("q", q_hbm.at[0], raw.at[0])
    fetch("fk", fk_hbm.at[0], raw.at[1])
    fetch("fv", fv_hbm.at[0, :, columns(x)], fvbuf.at[0])
    fetch("tk", tk_hbm.at[0, :, columns(x)], tkbuf)
    fetch("tv", tv_hbm.at[0, :, columns(x)], tvbuf)
    fetch("shift", shift_hbm, shiftbuf)
    fetch("scale", scale_hbm, scalebuf)
    fetch("proj", proj_hbm, projbuf)

    barrier = pltpu.get_barrier_semaphore()
    friends = [at(z, owner(d), core) for d in range(1, NX)] + [up, down, sibling, partner]
    for friend in friends:
        pl.semaphore_signal(barrier, inc=1, device_id=friend, device_id_type=MESH)
    pl.semaphore_wait(barrier, len(friends))

    for name, hbm, buf in (("sk", sk_hbm, kbuf), ("sv", sv_hbm, vbuf)):
        for d in range(1, NX):
            send(
                ("in", name, d),
                hbm.at[0, :, columns(owner(d))],
                buf.at[0, 0, d],
                at(z, owner(d), core),
            )

    def spread(kv, buf, d):
        send(("z", kv, 1, d), buf.at[0, 0, d], buf.at[1, 0, d], up)
        send(("z", kv, nz - 1, d), buf.at[0, 0, d], buf.at[nz - 1, 0, d], down)
        send(("s", kv, 0, d), buf.at[0, 0, d], buf.at[0, 1, d], sibling)

    locals_["sk"].wait()
    spread("k", kbuf, 0)
    locals_["sv"].wait()
    spread("v", vbuf, 0)

    at_row = lax.broadcasted_iota(jnp.int32, (rows, rows), 0)
    at_col = lax.broadcasted_iota(jnp.int32, (rows, rows), 1)
    places = pos_ref[...].astype(F32)
    angles = jnp.zeros((rows, HEAD_DIM), F32)
    for axis in range(3):
        column = jnp.sum(
            jnp.where(at_row == at_col, places[axis : axis + 1, :], 0.0), axis=1, keepdims=True
        )
        angles = angles + column * freq_ref[axis : axis + 1, :]
    even = lax.rem(lax.broadcasted_iota(jnp.int32, (rows, HEAD_DIM), 1), 2) == 0
    cosine = jnp.cos(angles)
    sine = jnp.sin(angles)
    sine = jnp.where(even, -sine, sine)
    locals_["q"].wait()
    locals_["fk"].wait()
    for which, name, sendbuf, ownbuf in ((0, "q", qsend, qbuf), (1, "fk", fksend, fkbuf)):
        for d in range(NX):
            for h in range(GROUP_HEADS):
                lanes = pl.ds(pl.multiple_of(owner(d) * GW + h * HEAD_DIM, 128), HEAD_DIM)
                value = raw[which, :, lanes].astype(F32)
                other = jnp.where(
                    even,
                    pltpu.roll(value, HEAD_DIM - 1, 1),
                    pltpu.roll(value, 1, 1),
                )
                turned = (value * cosine + other * sine).astype(BF16)
                target = ownbuf if d == 0 else sendbuf
                target[max(d - 1, 0) if d else 0, :, h * HEAD_DIM : (h + 1) * HEAD_DIM] = turned
            if d:
                send(("in", name, d), sendbuf.at[d - 1], ownbuf.at[d], at(z, owner(d), core))
    for d in range(1, NX):
        send(
            ("in", "fv", d),
            fv_hbm.at[0, :, columns(owner(d))],
            fvbuf.at[d],
            at(z, owner(d), core),
        )

    for name, kv, buf in (("sk", "k", kbuf), ("sv", "v", vbuf)):
        for d in range(1, NX):
            arrived(("in", name, d))
            spread(kv, buf, d)

    def lanes_of(h):
        return slice(h * HEAD_DIM, (h + 1) * HEAD_DIM)

    def stacked(buf, h, slots):
        pieces = [
            buf[slot + (d,)][:, lanes_of(h)].astype(F32) for slot in slots for d in range(NX)
        ]
        return jnp.concatenate(pieces, axis=0).astype(BF16)

    def scores_of(h, tile):
        return lax.dot_general(
            qh[h], tile, (((1,), (1,)), ((), ())), preferred_element_type=F32
        )

    def weigh(weights, tile):
        return jnp.dot(weights.astype(BF16), tile, preferred_element_type=F32)

    all_rows = NX * rows
    for d in range(1, NX):
        arrived(("in", "q", d))
    for h in range(GROUP_HEADS):
        qh[h] = stacked(qbuf, h, [()])
    for d in range(1, NX):
        arrived(("in", "fk", d))
        arrived(("in", "fv", d))
    locals_["fv"].wait()
    locals_["tk"].wait()
    locals_["tv"].wait()
    block_row = lax.broadcasted_iota(jnp.int32, (all_rows, all_rows), 0) // rows
    block_col = lax.broadcasted_iota(jnp.int32, (all_rows, all_rows), 1) // rows
    same = block_row == block_col
    words = tkbuf.shape[0]
    live = lax.broadcasted_iota(jnp.int32, (all_rows, words), 1) < cnt_ref[0]
    for h in range(GROUP_HEADS):
        own = jnp.where(
            same,
            scores_of(h, stacked(fkbuf, h, [()])),
            scores_of(h, stacked(kbuf, h, [(0, 0)])),
        )
        word = jnp.where(live, scores_of(h, tkbuf[:, lanes_of(h)]), -jnp.inf)
        high = jnp.maximum(
            jnp.max(own, axis=1, keepdims=True), jnp.max(word, axis=1, keepdims=True)
        )
        own = jnp.exp2((own - high) * SCALE2)
        word = jnp.exp2((word - high) * SCALE2)
        top[h] = high
        total[h] = jnp.sum(own, axis=1, keepdims=True) + jnp.sum(word, axis=1, keepdims=True)
        acc[h] = (
            weigh(jnp.where(same, own, 0.0), stacked(fvbuf, h, [()]))
            + weigh(jnp.where(same, 0.0, own), stacked(vbuf, h, [(0, 0)]))
            + weigh(word, tvbuf[:, lanes_of(h)])
        )

    def absorb(slots):
        for h in range(GROUP_HEADS):
            score = scores_of(h, stacked(kbuf, h, slots))
            old = top[h]
            high = jnp.maximum(old, jnp.max(score, axis=1, keepdims=True))
            weights = jnp.exp2((score - high) * SCALE2)
            rescale = jnp.exp2((old - high) * SCALE2)
            top[h] = high
            total[h] = total[h] * rescale + jnp.sum(weights, axis=1, keepdims=True)
            acc[h] = acc[h] * rescale + weigh(weights, stacked(vbuf, h, slots))

    def sibling_arrived(r):
        for kv in ("k", "v"):
            if r == 0:
                for d in range(NX):
                    arrived(("s", kv, 0, d))
            else:
                arrived(("s", kv, r))

    pending = [0]
    for t in range(1, half + 1):
        here = []
        for kv, buf in (("k", kbuf), ("v", vbuf)):
            for r, step, device in ((t, 1, up), (nz - t, -1, down)):
                if t == half and (kv == "k") != (step == 1):
                    continue
                if t == 1:
                    for d in range(NX):
                        arrived(("z", kv, r, d))
                else:
                    arrived(("z", kv, r))
                following = r + step
                last = following == half
                crossed = (r < half) == (step == 1) and r != half
                if crossed and (not last or (kv == "k") == (step == 1)):
                    send(("z", kv, following), buf.at[r, 0], buf.at[following, 0], device)
                send(("s", kv, r), buf.at[r, 0], buf.at[r, 1], sibling)
                if r not in here:
                    here.append(r)
        for r in pending:
            sibling_arrived(r)
        absorb([(r, 0) for r in here] + [(r, 1) for r in pending])
        pending = here
    for r in pending:
        sibling_arrived(r)
    absorb([(r, 1) for r in pending])

    for h in range(GROUP_HEADS):
        attended = acc[h] / total[h]
        for d in range(NX):
            osend[d, :, lanes_of(h)] = attended[d * rows : (d + 1) * rows, :]
    for d in range(1, NX):
        send(("o", d), osend.at[d], orecv.at[x], at(z, asker(d), core))
    orecv[x] = osend[0]
    for name in ("shift", "scale", "proj"):
        locals_[name].wait()
    for d in range(1, NX):
        arrived(("o", d))

    features = HEADS * HEAD_DIM
    parts = [orecv[g] for g in range(NX)]
    mean = sum(jnp.sum(part, axis=1, keepdims=True) for part in parts) / features
    parts = [part - mean for part in parts]
    spread_ = sum(jnp.sum(part * part, axis=1, keepdims=True) for part in parts) / features
    inverse = lax.rsqrt(spread_ + EPSILON)
    predicted = None
    for g in range(NX):
        wide = slice(g * GW, (g + 1) * GW)
        modulated = parts[g] * inverse * (1.0 + scalebuf[:, wide]) + shiftbuf[:, wide]
        term = jnp.dot(modulated.astype(BF16), projbuf[wide, :], preferred_element_type=F32)
        predicted = term if predicted is None else predicted + term
    width = predicted.shape[1] // 2
    low, high_half = predicted[:, :width], predicted[:, width:]
    first = branch == 0
    psend[...] = jnp.where(first, high_half, low)
    send(("cfg",), psend, precv, partner)
    keep = jnp.where(first, low, high_half)
    own_weight = jnp.where(first, 1.0 - GUIDANCE, GUIDANCE)
    other_weight = jnp.where(first, GUIDANCE, 1.0 - GUIDANCE)
    arrived(("cfg",))
    out_ref[0] = own_weight * keep + other_weight * precv[...]
    for copy in started.values():
        copy.wait_send()


def shards(nz, *args):
    (q, fk, fv, sk, sv, tk, tv, count, positions, shift, scale, proj) = args
    rows, features = q.shape[1], q.shape[2]
    words = tk.shape[1]
    width = proj.shape[1] // 2
    n_copies = len(copy_keys(nz))
    anywhere = pl.BlockSpec(memory_space=pl.ANY)
    in_vmem = pl.BlockSpec(memory_space=pltpu.VMEM)

    def body(*refs):
        kernel(nz, rows, *refs)

    return pl.pallas_call(
        body,
        out_shape=jax.ShapeDtypeStruct((1, rows, width), F32),
        in_specs=[anywhere] * 10
        + [pl.BlockSpec(memory_space=pltpu.SMEM), in_vmem, in_vmem],
        out_specs=in_vmem,
        scratch_shapes=[
            pltpu.VMEM((2, rows, features), BF16),
            pltpu.VMEM((NX - 1, rows, GW), BF16),
            pltpu.VMEM((NX - 1, rows, GW), BF16),
            pltpu.VMEM((NX, rows, GW), BF16),
            pltpu.VMEM((NX, rows, GW), BF16),
            pltpu.VMEM((NX, rows, GW), BF16),
            pltpu.VMEM((nz, NC, NX, rows, GW), BF16),
            pltpu.VMEM((nz, NC, NX, rows, GW), BF16),
            pltpu.VMEM((words, GW), BF16),
            pltpu.VMEM((words, GW), BF16),
            pltpu.VMEM((1, features), F32),
            pltpu.VMEM((1, features), F32),
            pltpu.VMEM((features, 2 * width), BF16),
            pltpu.VMEM((GROUP_HEADS, NX * rows, HEAD_DIM), BF16),
            pltpu.VMEM((GROUP_HEADS, NX * rows, 1), F32),
            pltpu.VMEM((GROUP_HEADS, NX * rows, 1), F32),
            pltpu.VMEM((GROUP_HEADS, NX * rows, HEAD_DIM), F32),
            pltpu.VMEM((NX, rows, GW), F32),
            pltpu.VMEM((NX, rows, GW), F32),
            pltpu.VMEM((rows, width), F32),
            pltpu.VMEM((rows, width), F32),
            pltpu.SemaphoreType.DMA((10,)),
            pltpu.SemaphoreType.DMA((n_copies,)),
            pltpu.SemaphoreType.DMA((n_copies,)),
        ],
        compiler_params=pltpu.CompilerParams(
            collective_id=0, has_side_effects=True, vmem_limit_bytes=48 * 1024 * 1024
        ),
        name="stale_attention",
    )(q, fk, fv, sk, sv, tk, tv, shift, scale, proj, count, positions, jnp.asarray(lane_frequencies()))


def solution(mesh):
    nz = mesh.shape["patch"] // (NX * NC)
    placed = (
        P("cfg", "patch", "rep"),
        P("cfg", "patch", "rep"),
        P("cfg", "patch", "rep"),
        P("cfg", "patch", "rep"),
        P("cfg", "patch", "rep"),
        P("cfg", "rep", None),
        P("cfg", "rep", None),
        P("cfg"),
        P("rep", "patch"),
        P("cfg", None),
        P("cfg", None),
        P(),
    )

    def run(*args):
        return shards(nz, *args)

    return jax.shard_map(
        run, mesh=mesh, in_specs=placed, out_specs=P("cfg", "patch", "rep"), check_vma=False
    )
```

```python
import math

import jax
import jax.numpy as jnp
import numpy as np
from jax import lax
from jax.experimental import pallas as pl
from jax.experimental.pallas import tpu as pltpu
from jax.sharding import PartitionSpec as P

HEADS = 12
HEAD_DIM = 128
GUIDANCE = 4.0
EPSILON = 1e-06

NX = 4
NC = 2
NEAREST = (1, 3, 2)
GROUP_HEADS = HEADS // NX
GW = GROUP_HEADS * HEAD_DIM
SCALE2 = math.log2(math.e) / math.sqrt(HEAD_DIM)
SIDE = 64
F32 = jnp.float32
BF16 = jnp.bfloat16
MESH = pl.DeviceIdType.MESH


def lane_frequencies():
    time_extent = HEAD_DIM // 8
    space_extent = (HEAD_DIM - time_extent) // 2
    rows = np.zeros((3, HEAD_DIM), np.float32)
    start = 0
    for axis, extent in enumerate((time_extent, space_extent, space_extent)):
        exponent = -np.arange(0, extent, 2).astype(np.float32) / np.float32(extent)
        frequency = (256.0 ** exponent.astype(np.float64)).astype(np.float32)
        rows[axis, start : start + extent] = np.repeat(frequency, 2)
        start += extent
    return rows


def copy_keys(nz):
    keys = [("in", name, d) for name in ("sk", "sv", "q", "fk", "fv") for d in range(1, NX)]
    for kv in ("k", "v"):
        for d in range(NX):
            keys += [("z", kv, 1, d), ("z", kv, nz - 1, d)]
        keys.append(("s", kv, 0))
        for r in range(1, nz):
            keys.append(("s", kv, r))
            if r not in (1, nz - 1):
                keys.append(("z", kv, r))
    keys += [("own", d) for d in range(1, NX)]
    keys += [("other", d) for d in range(NX)]
    return keys


def kernel(
    nz,
    rows,
    q_hbm,
    fk_hbm,
    fv_hbm,
    sk_hbm,
    sv_hbm,
    tk_hbm,
    tv_hbm,
    shift_hbm,
    scale_hbm,
    proj_hbm,
    pos_hbm,
    freq_hbm,
    cnt_ref,
    out_ref,
    raw,
    qsend,
    fksend,
    qbuf,
    fkbuf,
    fvbuf,
    kbuf,
    vbuf,
    tkbuf,
    tvbuf,
    shiftbuf,
    scalebuf,
    projbuf,
    pos_ref,
    freq_ref,
    qh,
    top,
    total,
    acc,
    ysend,
    yrecv,
    local_sem,
    send_sem,
    recv_sem,
):
    keys = {key: i for i, key in enumerate(copy_keys(nz))}
    half = nz // 2
    patch = lax.axis_index("patch")
    branch = lax.axis_index("cfg")
    core = lax.rem(patch, NC)
    x = lax.rem(patch // NC, NX)
    z = patch // (NC * NX)

    def at(zz, xx, cc):
        return {"patch": (zz * NX + xx) * NC + cc}

    def owner(d):
        return lax.rem(x + NX - d, NX)

    def asker(d):
        return lax.rem(x + d, NX)

    up = at(lax.rem(z + 1, nz), x, core)
    down = at(lax.rem(z + nz - 1, nz), x, core)
    sibling = at(z, x, 1 - core)

    def across(xx):
        return {"cfg": 1 - branch, **at(z, xx, core)}

    started = {}

    def send(key, src, dst, device):
        i = keys[key]
        copy = pltpu.make_async_remote_copy(
            src_ref=src,
            dst_ref=dst,
            send_sem=send_sem.at[i],
            recv_sem=recv_sem.at[i],
            device_id=device,
            device_id_type=MESH,
        )
        copy.start()
        started[key] = copy

    def arrived(key):
        started[key].wait_recv()

    locals_ = {}

    def fetch(name, src, dst):
        copy = pltpu.make_async_copy(src, dst, local_sem.at[len(locals_)])
        copy.start()
        locals_[name] = copy

    def columns(group):
        return pl.ds(pl.multiple_of(group * GW, 128), GW)

    fetch("pos", pos_hbm, pos_ref)
    fetch("freq", freq_hbm, freq_ref)
    fetch("sk", sk_hbm.at[0, :, columns(x)], kbuf.at[0, 0, 0])
    fetch("sv", sv_hbm.at[0, :, columns(x)], vbuf.at[0, 0, 0])
    fetch("q", q_hbm.at[0], raw.at[0])
    fetch("fk", fk_hbm.at[0], raw.at[1])
    fetch("fv", fv_hbm.at[0, :, columns(x)], fvbuf.at[0])
    fetch("tk", tk_hbm.at[0, :, columns(x)], tkbuf)
    fetch("tv", tv_hbm.at[0, :, columns(x)], tvbuf)
    fetch("shift", shift_hbm.at[:, columns(x)], shiftbuf)
    fetch("scale", scale_hbm.at[:, columns(x)], scalebuf)
    fetch("proj", proj_hbm.at[:, columns(x)], projbuf)

    barrier = pltpu.get_barrier_semaphore()
    friends = [at(z, owner(d), core) for d in range(1, NX)] + [up, down, sibling]
    friends += [across(owner(d)) for d in range(NX)]
    for friend in friends:
        pl.semaphore_signal(barrier, inc=1, device_id=friend, device_id_type=MESH)
    pl.semaphore_wait(barrier, len(friends))

    for name, hbm, buf in (("sk", sk_hbm, kbuf), ("sv", sv_hbm, vbuf)):
        for d in NEAREST:
            send(
                ("in", name, d),
                hbm.at[0, :, columns(owner(d))],
                buf.at[0, 0, d],
                at(z, owner(d), core),
            )

    def spread(kv, buf, d):
        send(("z", kv, 1, d), buf.at[0, 0, d], buf.at[1, 0, d], up)
        send(("z", kv, nz - 1, d), buf.at[0, 0, d], buf.at[nz - 1, 0, d], down)

    locals_["sk"].wait()
    spread("k", kbuf, 0)
    locals_["sv"].wait()
    spread("v", vbuf, 0)

    at_row = lax.broadcasted_iota(jnp.int32, (rows, rows), 0)
    at_col = lax.broadcasted_iota(jnp.int32, (rows, rows), 1)
    locals_["pos"].wait()
    locals_["freq"].wait()
    places = pos_ref[...].astype(F32)
    angles = jnp.zeros((rows, HEAD_DIM), F32)
    for axis in range(3):
        column = jnp.sum(
            jnp.where(at_row == at_col, places[axis : axis + 1, :], 0.0), axis=1, keepdims=True
        )
        angles = angles + column * freq_ref[axis : axis + 1, :]
    even = lax.rem(lax.broadcasted_iota(jnp.int32, (rows, HEAD_DIM), 1), 2) == 0
    cosine = jnp.cos(angles)
    sine = jnp.sin(angles)
    sine = jnp.where(even, -sine, sine)
    locals_["q"].wait()
    locals_["fk"].wait()
    for which, name, sendbuf, ownbuf in ((0, "q", qsend, qbuf), (1, "fk", fksend, fkbuf)):
        for d in range(NX):
            for h in range(GROUP_HEADS):
                lanes = pl.ds(pl.multiple_of(owner(d) * GW + h * HEAD_DIM, 128), HEAD_DIM)
                value = raw[which, :, lanes].astype(F32)
                other = jnp.where(
                    even,
                    pltpu.roll(value, HEAD_DIM - 1, 1),
                    pltpu.roll(value, 1, 1),
                )
                turned = (value * cosine + other * sine).astype(BF16)
                target = ownbuf if d == 0 else sendbuf
                target[max(d - 1, 0) if d else 0, :, h * HEAD_DIM : (h + 1) * HEAD_DIM] = turned

    for name, kv, buf in (("sk", "k", kbuf), ("sv", "v", vbuf)):
        for d in NEAREST:
            arrived(("in", name, d))
            spread(kv, buf, d)
    for kv, buf in (("k", kbuf), ("v", vbuf)):
        send(("s", kv, 0), buf.at[0, 0], buf.at[0, 1], sibling)
    for d in NEAREST:
        send(("in", "q", d), qsend.at[d - 1], qbuf.at[d], at(z, owner(d), core))
    for d in NEAREST:
        send(("in", "fk", d), fksend.at[d - 1], fkbuf.at[d], at(z, owner(d), core))
        send(
            ("in", "fv", d),
            fv_hbm.at[0, :, columns(owner(d))],
            fvbuf.at[d],
            at(z, owner(d), core),
        )

    def lanes_of(h):
        return slice(h * HEAD_DIM, (h + 1) * HEAD_DIM)

    def stacked(buf, h, slots):
        pieces = [
            buf[slot + (d,)][:, lanes_of(h)].astype(F32) for slot in slots for d in range(NX)
        ]
        return jnp.concatenate(pieces, axis=0).astype(BF16)

    def scores_of(h, tile):
        return lax.dot_general(
            qh[h], tile, (((1,), (1,)), ((), ())), preferred_element_type=F32
        )

    def weigh(weights, tile):
        return jnp.dot(weights.astype(BF16), tile, preferred_element_type=F32)

    all_rows = NX * rows

    def begin():
        for d in range(1, NX):
            arrived(("in", "q", d))
        for h in range(GROUP_HEADS):
            qh[h] = stacked(qbuf, h, [()])
        for d in range(1, NX):
            arrived(("in", "fk", d))
            arrived(("in", "fv", d))
        locals_["fv"].wait()
        locals_["tk"].wait()
        locals_["tv"].wait()
        block_row = lax.broadcasted_iota(jnp.int32, (all_rows, all_rows), 0) // rows
        block_col = lax.broadcasted_iota(jnp.int32, (all_rows, all_rows), 1) // rows
        same = block_row == block_col
        words = tkbuf.shape[0]
        live = lax.broadcasted_iota(jnp.int32, (all_rows, words), 1) < cnt_ref[0]
        for h in range(GROUP_HEADS):
            own = jnp.where(
                same,
                scores_of(h, stacked(fkbuf, h, [()])),
                scores_of(h, stacked(kbuf, h, [(0, 0)])),
            )
            word = jnp.where(live, scores_of(h, tkbuf[:, lanes_of(h)]), -jnp.inf)
            high = jnp.maximum(
                jnp.max(own, axis=1, keepdims=True), jnp.max(word, axis=1, keepdims=True)
            )
            own = jnp.exp2((own - high) * SCALE2)
            word = jnp.exp2((word - high) * SCALE2)
            top[h] = high
            total[h] = jnp.sum(own, axis=1, keepdims=True) + jnp.sum(word, axis=1, keepdims=True)
            acc[h] = (
                weigh(jnp.where(same, own, 0.0), stacked(fvbuf, h, [()]))
                + weigh(jnp.where(same, 0.0, own), stacked(vbuf, h, [(0, 0)]))
                + weigh(word, tvbuf[:, lanes_of(h)])
            )


    def absorb(slots):
        for h in range(GROUP_HEADS):
            score = scores_of(h, stacked(kbuf, h, slots))
            old = top[h]
            high = jnp.maximum(old, jnp.max(score, axis=1, keepdims=True))
            weights = jnp.exp2((score - high) * SCALE2)
            rescale = jnp.exp2((old - high) * SCALE2)
            top[h] = high
            total[h] = total[h] * rescale + jnp.sum(weights, axis=1, keepdims=True)
            acc[h] = acc[h] * rescale + weigh(weights, stacked(vbuf, h, slots))

    def sibling_arrived(r):
        for kv in ("k", "v"):
            arrived(("s", kv, r))

    pending = [0]
    for t in range(1, half + 1):
        if t == half:
            for r in pending:
                sibling_arrived(r)
            absorb([(r, 1) for r in pending])
            pending = []
        here = []
        for kv, buf in (("k", kbuf), ("v", vbuf)):
            for r, step, device in ((t, 1, up), (nz - t, -1, down)):
                if t == half and (kv == "k") != (step == 1):
                    continue
                if t == 1:
                    for d in range(NX):
                        arrived(("z", kv, r, d))
                else:
                    arrived(("z", kv, r))
                following = r + step
                if t < half and (following != half or (kv == "k") == (step == 1)):
                    send(("z", kv, following), buf.at[r, 0], buf.at[following, 0], device)
                if r not in here:
                    here.append(r)
            for r in here:
                send(("s", kv, r), buf.at[r, 0], buf.at[r, 1], sibling)
        if t == 1:
            begin()
        for r in pending:
            sibling_arrived(r)
        absorb([(r, 0) for r in here] + [(r, 1) for r in pending])
        pending = here
    for r in pending:
        sibling_arrived(r)
    absorb([(r, 1) for r in pending])

    for name in ("shift", "scale", "proj"):
        locals_[name].wait()
    width = projbuf.shape[0] // 2
    gap = jnp.zeros((SIDE - width, GW), BF16)
    channels = jnp.concatenate([projbuf[:width], gap, projbuf[width:], gap], axis=0)

    def project(value, h):
        tile = channels[:, lanes_of(h)]
        big = value.astype(BF16)
        small = (value - big.astype(F32)).astype(BF16)
        nt = (((1,), (1,)), ((), ()))
        return lax.dot_general(
            big, tile, nt, preferred_element_type=F32
        ) + lax.dot_general(small, tile, nt, preferred_element_type=F32)

    gain = 1.0 + scalebuf[...]
    affine = jnp.concatenate([gain, shiftbuf[...], jnp.zeros((6, GW), F32)], axis=0)
    affine = sum(project(affine[:, lanes_of(h)], h) for h in range(GROUP_HEADS))
    attended = [acc[h] / total[h] for h in range(GROUP_HEADS)]
    mean = sum(jnp.sum(part, axis=1, keepdims=True) for part in attended) / GW
    attended = [part - mean for part in attended]
    squares = sum(jnp.sum(part * part, axis=1, keepdims=True) for part in attended)
    share = sum(project(attended[h] * gain[:, lanes_of(h)], h) for h in range(GROUP_HEADS))
    lane = lax.rem(lax.broadcasted_iota(jnp.int32, share.shape, 1), SIDE)
    share = jnp.where(lane == width, mean, jnp.where(lane == width + 1, squares, share))
    for d in range(NX):
        ysend[d, :rows] = share[d * rows : (d + 1) * rows]
        ysend[d, rows:] = affine
    for d in NEAREST:
        send(("own", d), ysend.at[d], yrecv.at[0, d], at(z, asker(d), core))
    for d in (0,) + NEAREST:
        send(("other", d), ysend.at[d], yrecv.at[1, d], across(asker(d)))
    yrecv[0, 0] = ysend[0]
    for d in NEAREST:
        arrived(("own", d))
    for d in range(NX):
        arrived(("other", d))

    def prediction(side):
        blocks = [yrecv[side, d] for d in range(NX)]
        means = [block[:rows, width : width + 1] for block in blocks]
        middle = sum(means) / NX
        spread_ = sum(block[:rows, width + 1 : width + 2] for block in blocks)
        spread_ = spread_ + GW * sum((mean_ - middle) * (mean_ - middle) for mean_ in means)
        inverse = lax.rsqrt(spread_ / (NX * GW) + EPSILON)
        linear = sum(
            block[:rows] + (mean_ - middle) * block[rows : rows + 1]
            for block, mean_ in zip(blocks, means)
        )
        return inverse * linear + sum(block[rows + 1 : rows + 2] for block in blocks)

    first = branch == 0
    own_weight = jnp.where(first, 1.0 - GUIDANCE, GUIDANCE)
    other_weight = jnp.where(first, GUIDANCE, 1.0 - GUIDANCE)
    guided = (own_weight * prediction(0) + other_weight * prediction(1)).T
    out_ref[0] = jnp.where(first, guided[:width], guided[SIDE : SIDE + width])
    for copy in started.values():
        copy.wait_send()


def shards(nz, *args):
    (q, fk, fv, sk, sv, tk, tv, count, positions, shift, scale, proj) = args
    rows, features = q.shape[1], q.shape[2]
    words = tk.shape[1]
    width = proj.shape[1] // 2
    n_copies = len(copy_keys(nz))
    anywhere = pl.BlockSpec(memory_space=pl.ANY)
    in_vmem = pl.BlockSpec(memory_space=pltpu.VMEM)

    def body(*refs):
        kernel(nz, rows, *refs)

    guided = pl.pallas_call(
        body,
        out_shape=jax.ShapeDtypeStruct((1, width, rows), F32),
        in_specs=[anywhere] * 12 + [pl.BlockSpec(memory_space=pltpu.SMEM)],
        out_specs=in_vmem,
        scratch_shapes=[
            pltpu.VMEM((2, rows, features), BF16),
            pltpu.VMEM((NX - 1, rows, GW), BF16),
            pltpu.VMEM((NX - 1, rows, GW), BF16),
            pltpu.VMEM((NX, rows, GW), BF16),
            pltpu.VMEM((NX, rows, GW), BF16),
            pltpu.VMEM((NX, rows, GW), BF16),
            pltpu.VMEM((nz, NC, NX, rows, GW), BF16),
            pltpu.VMEM((nz, NC, NX, rows, GW), BF16),
            pltpu.VMEM((words, GW), BF16),
            pltpu.VMEM((words, GW), BF16),
            pltpu.VMEM((1, GW), F32),
            pltpu.VMEM((1, GW), F32),
            pltpu.VMEM((2 * width, GW), BF16),
            pltpu.VMEM((3, rows), jnp.int32),
            pltpu.VMEM((3, HEAD_DIM), F32),
            pltpu.VMEM((GROUP_HEADS, NX * rows, HEAD_DIM), BF16),
            pltpu.VMEM((GROUP_HEADS, NX * rows, 1), F32),
            pltpu.VMEM((GROUP_HEADS, NX * rows, 1), F32),
            pltpu.VMEM((GROUP_HEADS, NX * rows, HEAD_DIM), F32),
            pltpu.VMEM((NX, rows + 8, 2 * SIDE), F32),
            pltpu.VMEM((2, NX, rows + 8, 2 * SIDE), F32),
            pltpu.SemaphoreType.DMA((12,)),
            pltpu.SemaphoreType.DMA((n_copies,)),
            pltpu.SemaphoreType.DMA((n_copies,)),
        ],
        compiler_params=pltpu.CompilerParams(
            collective_id=0, has_side_effects=True, vmem_limit_bytes=62 * 1024 * 1024
        ),
        name="stale_attention",
    )(
        q, fk, fv, sk, sv, tk, tv, shift, scale, proj.T, positions, jnp.asarray(lane_frequencies()), count
    )
    return jnp.swapaxes(guided, 1, 2)


def solution(mesh):
    nz = mesh.shape["patch"] // (NX * NC)
    placed = (
        P("cfg", "patch", "rep"),
        P("cfg", "patch", "rep"),
        P("cfg", "patch", "rep"),
        P("cfg", "patch", "rep"),
        P("cfg", "patch", "rep"),
        P("cfg", "rep", None),
        P("cfg", "rep", None),
        P("cfg"),
        P("rep", "patch"),
        P("cfg", None),
        P("cfg", None),
        P(),
    )

    def run(*args):
        return shards(nz, *args)

    return jax.shard_map(
        run, mesh=mesh, in_specs=placed, out_specs=P("cfg", "patch", "rep"), check_vma=False
    )
```

```python
import math

import jax
import jax.numpy as jnp
import numpy as np
from jax import lax
from jax.experimental import pallas as pl
from jax.experimental.pallas import tpu as pltpu
from jax.sharding import PartitionSpec as P

HEADS = 12
HEAD_DIM = 128
GUIDANCE = 4.0
EPSILON = 1e-06

NX = 4
NC = 2
NEAREST = (1, 3, 2)
GROUP_HEADS = HEADS // NX
GW = GROUP_HEADS * HEAD_DIM
SCALE2 = math.log2(math.e) / math.sqrt(HEAD_DIM)
SIDE = 64
PACK = 16
STEP = 40
F32 = jnp.float32
BF16 = jnp.bfloat16
MESH = pl.DeviceIdType.MESH


def lane_frequencies():
    time_extent = HEAD_DIM // 8
    space_extent = (HEAD_DIM - time_extent) // 2
    rows = np.zeros((3, HEAD_DIM), np.float32)
    start = 0
    for axis, extent in enumerate((time_extent, space_extent, space_extent)):
        exponent = -np.arange(0, extent, 2).astype(np.float32) / np.float32(extent)
        frequency = (256.0 ** exponent.astype(np.float64)).astype(np.float32)
        rows[axis, start : start + extent] = np.repeat(frequency, 2)
        start += extent
    return rows


def copy_keys(nz):
    keys = [("in", name, d) for name in ("sk", "sv", "q", "fk", "fv") for d in range(1, NX)]
    for kv in ("k", "v"):
        for d in range(NX):
            keys += [("z", kv, 1, d), ("z", kv, nz - 1, d)]
        keys.append(("s", kv, 0))
        for r in range(1, nz):
            keys.append(("s", kv, r))
            if r not in (1, nz - 1):
                keys.append(("z", kv, r))
    keys += [("own", d) for d in range(1, NX)]
    keys += [("other", d) for d in range(NX)]
    return keys


def kernel(
    nz,
    rows,
    q_hbm,
    fk_hbm,
    fv_hbm,
    sk_hbm,
    sv_hbm,
    tk_hbm,
    tv_hbm,
    shift_hbm,
    scale_hbm,
    proj_hbm,
    pos_hbm,
    freq_hbm,
    cnt_ref,
    out_ref,
    raw,
    qsend,
    fksend,
    qbuf,
    fkbuf,
    fvbuf,
    kbuf,
    vbuf,
    tkbuf,
    tvbuf,
    shiftbuf,
    scalebuf,
    projbuf,
    pos_ref,
    freq_ref,
    qh,
    top,
    total,
    acc,
    ysend,
    yrecv,
    local_sem,
    send_sem,
    recv_sem,
):
    keys = {key: i for i, key in enumerate(copy_keys(nz))}
    half = nz // 2
    patch = lax.axis_index("patch")
    branch = lax.axis_index("cfg")
    core = lax.rem(patch, NC)
    x = lax.rem(patch // NC, NX)
    z = patch // (NC * NX)

    def at(zz, xx, cc):
        return {"patch": (zz * NX + xx) * NC + cc}

    def owner(d):
        return lax.rem(x + NX - d, NX)

    def asker(d):
        return lax.rem(x + d, NX)

    up = at(lax.rem(z + 1, nz), x, core)
    down = at(lax.rem(z + nz - 1, nz), x, core)
    sibling = at(z, x, 1 - core)

    def across(xx):
        return {"cfg": 1 - branch, **at(z, xx, core)}

    started = {}

    def send(key, src, dst, device):
        i = keys[key]
        copy = pltpu.make_async_remote_copy(
            src_ref=src,
            dst_ref=dst,
            send_sem=send_sem.at[i],
            recv_sem=recv_sem.at[i],
            device_id=device,
            device_id_type=MESH,
        )
        copy.start()
        started[key] = copy

    def arrived(key):
        started[key].wait_recv()

    locals_ = {}

    def fetch(name, src, dst):
        copy = pltpu.make_async_copy(src, dst, local_sem.at[len(locals_)])
        copy.start()
        locals_[name] = copy

    def columns(group):
        return pl.ds(pl.multiple_of(group * GW, 128), GW)

    barrier = pltpu.get_barrier_semaphore()
    friends = [at(z, owner(d), core) for d in range(1, NX)] + [up, down, sibling]
    friends += [across(owner(d)) for d in range(NX)]
    for friend in friends:
        pl.semaphore_signal(barrier, inc=1, device_id=friend, device_id_type=MESH)
    pl.semaphore_wait(barrier, len(friends))

    for name, hbm, buf in (("sk", sk_hbm, kbuf), ("sv", sv_hbm, vbuf)):
        for d in NEAREST:
            send(
                ("in", name, d),
                hbm.at[0, :, columns(owner(d))],
                buf.at[0, 0, d],
                at(z, owner(d), core),
            )

    def spread(kv, src, buf, d):
        send(("z", kv, 1, d), src, buf.at[1, 0, d], up)
        send(("z", kv, nz - 1, d), src, buf.at[nz - 1, 0, d], down)

    spread("k", sk_hbm.at[0, :, columns(x)], kbuf, 0)
    spread("v", sv_hbm.at[0, :, columns(x)], vbuf, 0)

    fetch("pos", pos_hbm, pos_ref)
    fetch("freq", freq_hbm, freq_ref)
    fetch("sk", sk_hbm.at[0, :, columns(x)], kbuf.at[0, 0, 0])
    fetch("sv", sv_hbm.at[0, :, columns(x)], vbuf.at[0, 0, 0])
    fetch("q", q_hbm.at[0], raw.at[0])
    fetch("fk", fk_hbm.at[0], raw.at[1])
    fetch("fv", fv_hbm.at[0, :, columns(x)], fvbuf.at[0])
    fetch("tk", tk_hbm.at[0, :, columns(x)], tkbuf)
    fetch("tv", tv_hbm.at[0, :, columns(x)], tvbuf)
    fetch("shift", shift_hbm.at[:, columns(x)], shiftbuf)
    fetch("scale", scale_hbm.at[:, columns(x)], scalebuf)
    fetch("proj", proj_hbm.at[:, columns(x)], projbuf)

    for name, kv, buf in (("sk", "k", kbuf), ("sv", "v", vbuf)):
        for d in NEAREST:
            arrived(("in", name, d))
            spread(kv, buf.at[0, 0, d], buf, d)
    for kv, buf in (("k", kbuf), ("v", vbuf)):
        locals_["s" + kv].wait()
        send(("s", kv, 0), buf.at[0, 0], buf.at[0, 1], sibling)
    at_row = lax.broadcasted_iota(jnp.int32, (rows, rows), 0)
    at_col = lax.broadcasted_iota(jnp.int32, (rows, rows), 1)
    locals_["pos"].wait()
    locals_["freq"].wait()
    places = pos_ref[...].astype(F32)
    angles = jnp.zeros((rows, HEAD_DIM), F32)
    for axis in range(3):
        column = jnp.sum(
            jnp.where(at_row == at_col, places[axis : axis + 1, :], 0.0), axis=1, keepdims=True
        )
        angles = angles + column * freq_ref[axis : axis + 1, :]
    even = lax.rem(lax.broadcasted_iota(jnp.int32, (rows, HEAD_DIM), 1), 2) == 0
    cosine = jnp.cos(angles)
    sine = jnp.sin(angles)
    sine = jnp.where(even, -sine, sine)
    locals_["q"].wait()
    locals_["fk"].wait()
    for which, name, sendbuf, ownbuf in ((0, "q", qsend, qbuf), (1, "fk", fksend, fkbuf)):
        for d in range(NX):
            for h in range(GROUP_HEADS):
                lanes = pl.ds(pl.multiple_of(owner(d) * GW + h * HEAD_DIM, 128), HEAD_DIM)
                value = raw[which, :, lanes].astype(F32)
                other = jnp.where(
                    even,
                    pltpu.roll(value, HEAD_DIM - 1, 1),
                    pltpu.roll(value, 1, 1),
                )
                turned = (value * cosine + other * sine).astype(BF16)
                target = ownbuf if d == 0 else sendbuf
                target[max(d - 1, 0) if d else 0, :, h * HEAD_DIM : (h + 1) * HEAD_DIM] = turned

    for d in NEAREST:
        send(("in", "q", d), qsend.at[d - 1], qbuf.at[d], at(z, owner(d), core))
    for d in NEAREST:
        send(("in", "fk", d), fksend.at[d - 1], fkbuf.at[d], at(z, owner(d), core))
        send(
            ("in", "fv", d),
            fv_hbm.at[0, :, columns(owner(d))],
            fvbuf.at[d],
            at(z, owner(d), core),
        )

    def lanes_of(h):
        return slice(h * HEAD_DIM, (h + 1) * HEAD_DIM)

    def stacked(buf, h, slots):
        pieces = [
            buf[slot + (d,)][:, lanes_of(h)].astype(F32) for slot in slots for d in range(NX)
        ]
        return jnp.concatenate(pieces, axis=0).astype(BF16)

    def scores_of(h, tile):
        return lax.dot_general(
            qh[h], tile, (((1,), (1,)), ((), ())), preferred_element_type=F32
        )

    def weigh(weights, tile):
        wide = jnp.concatenate([tile, jnp.ones_like(tile)], axis=1)
        return jnp.dot(weights.astype(BF16), wide, preferred_element_type=F32)

    def largest(score):
        return jnp.broadcast_to(
            jnp.max(score, axis=1, keepdims=True), (score.shape[0], HEAD_DIM)
        )

    def relative(score, high):
        copies = -(-score.shape[1] // HEAD_DIM)
        wide = jnp.concatenate([high] * copies, axis=1)[:, : score.shape[1]]
        return jnp.exp2((score - wide) * SCALE2)

    all_rows = NX * rows

    def begin():
        for d in range(1, NX):
            arrived(("in", "q", d))
        for h in range(GROUP_HEADS):
            qh[h] = stacked(qbuf, h, [()])
        for d in range(1, NX):
            arrived(("in", "fk", d))
            arrived(("in", "fv", d))
        locals_["fv"].wait()
        locals_["tk"].wait()
        locals_["tv"].wait()
        block_row = lax.broadcasted_iota(jnp.int32, (all_rows, all_rows), 0) // rows
        block_col = lax.broadcasted_iota(jnp.int32, (all_rows, all_rows), 1) // rows
        same = block_row == block_col
        words = tkbuf.shape[0]
        live = lax.broadcasted_iota(jnp.int32, (all_rows, words), 1) < cnt_ref[0]
        for h in range(GROUP_HEADS):
            own = jnp.where(
                same,
                scores_of(h, stacked(fkbuf, h, [()])),
                scores_of(h, stacked(kbuf, h, [(0, 0)])),
            )
            word = jnp.where(live, scores_of(h, tkbuf[:, lanes_of(h)]), -jnp.inf)
            high = jnp.maximum(largest(own), largest(word))
            own = relative(own, high)
            word = relative(word, high)
            top[h] = high
            summed = (
                weigh(jnp.where(same, own, 0.0), stacked(fvbuf, h, [()]))
                + weigh(jnp.where(same, 0.0, own), stacked(vbuf, h, [(0, 0)]))
                + weigh(word, tvbuf[:, lanes_of(h)])
            )
            acc[h] = summed[:, :HEAD_DIM]
            total[h] = summed[:, HEAD_DIM:]

    def absorbed(h, slots):
        score = scores_of(h, stacked(kbuf, h, slots))
        old = top[h]
        high = jnp.maximum(old, largest(score))
        summed = weigh(relative(score, high), stacked(vbuf, h, slots))
        rescale = jnp.exp2((old - high) * SCALE2)
        return (
            high,
            total[h] * rescale + summed[:, HEAD_DIM:],
            acc[h] * rescale + summed[:, :HEAD_DIM],
        )

    def absorb(slots):
        for h in range(GROUP_HEADS):
            top[h], total[h], acc[h] = absorbed(h, slots)

    def sibling_arrived(r):
        for kv in ("k", "v"):
            arrived(("s", kv, r))

    first = branch == 0
    width = projbuf.shape[0] // 2

    def project(value, tile):
        big = value.astype(BF16)
        small = (value - big.astype(F32)).astype(BF16)
        nt = (((1,), (1,)), ((), ()))
        return lax.dot_general(
            big, tile, nt, preferred_element_type=F32
        ) + lax.dot_general(small, tile, nt, preferred_element_type=F32)

    def forward(kv, buf, t):
        for r, step, device in ((t, 1, up), (nz - t, -1, down)):
            if t == 1:
                for d in range(NX):
                    arrived(("z", kv, r, d))
            else:
                arrived(("z", kv, r))
            following = r + step
            if following != half or (kv == "k") == (step == 1):
                send(("z", kv, following), buf.at[r, 0], buf.at[following, 0], device)
        for r in (t, nz - t):
            send(("s", kv, r), buf.at[r, 0], buf.at[r, 1], sibling)

    both = (("k", kbuf), ("v", vbuf))
    backlog = []
    for t in range(1, half):
        for kv, buf in both:
            forward(kv, buf, t)
            if t == 2 and kv == "k":
                begin()
            elif t >= 2:
                for slot in backlog:
                    if slot[1] == 1:
                        sibling_arrived(slot[0])
                for i in range(0, len(backlog), 4):
                    absorb(backlog[i : i + 4])
                backlog = []
            if kv == "v":
                backlog += [(r, s) for s in (0, 1) for r in (t, nz - t)]
                if t == 1:
                    backlog += [(0, 1)]
    if half == 2:
        begin()
    for name in ("shift", "scale", "proj"):
        locals_[name].wait()
    low, high_half = projbuf[:width], projbuf[width:]
    gap = jnp.zeros((SIDE - width, GW), BF16)
    channels = jnp.concatenate(
        [jnp.where(first, low, high_half), gap, jnp.where(first, high_half, low), gap], axis=0
    )
    gain = 1.0 + scalebuf[...]
    affine = project(
        jnp.concatenate([gain, shiftbuf[...], jnp.zeros((6, GW), F32)], axis=0), channels
    )
    early, late = backlog[:2], backlog[2:]
    absorb(early)
    for slot in late:
        sibling_arrived(slot[0])
    absorb(late)
    for kv, buf in both:
        arrived(("z", kv, half))
        send(("s", kv, half), buf.at[half, 0], buf.at[half, 1], sibling)
    absorb([(half, 0)])
    sibling_arrived(half)

    attended = []
    for h in range(GROUP_HEADS):
        _, totals, sums = absorbed(h, [(half, 1)])
        attended.append(sums / totals)
    mean = jnp.sum(sum(attended), axis=1, keepdims=True) / GW
    attended = [part - mean for part in attended]
    squares = jnp.sum(sum(part * part for part in attended), axis=1, keepdims=True)
    share = sum(
        project(attended[h] * gain[:, lanes_of(h)], channels[:, lanes_of(h)])
        for h in range(GROUP_HEADS)
    )
    lane = lax.rem(lax.broadcasted_iota(jnp.int32, share.shape, 1), SIDE)
    share = jnp.where(lane == width, mean, jnp.where(lane == width + 1, squares, share))
    slot = lax.broadcasted_iota(jnp.int32, (PACK, HEAD_DIM), 1) // STEP

    def turn(value, shift):
        return pltpu.roll(value, shift % HEAD_DIM, 1) if shift % HEAD_DIM else value

    for side, d in [(1, 2), (1, 1), (1, 3), (0, 2), (0, 1), (0, 3), (1, 0), (0, 0)]:
        block = share[d * rows : (d + 1) * rows]
        strips = [
            block[:PACK],
            block[PACK : 2 * PACK],
            jnp.concatenate([block[2 * PACK :], affine], axis=0),
        ]
        strips = [turn(strip, i * STEP - side * SIDE) for i, strip in enumerate(strips)]
        packed = jnp.where(slot == 0, strips[0], jnp.where(slot == 1, strips[1], strips[2]))
        if (side, d) == (0, 0):
            yrecv[0, 0] = packed
        else:
            ysend[side, d] = packed
            if side:
                send(("other", d), ysend.at[1, d], yrecv.at[1, d], across(asker(d)))
            else:
                send(("own", d), ysend.at[0, d], yrecv.at[0, d], at(z, asker(d), core))

    def prediction(side):
        blocks = []
        for d in range(NX):
            packed = yrecv[side, d]
            blocks.append(
                jnp.concatenate([packed, turn(packed, -STEP), turn(packed, -2 * STEP)], axis=0)
            )
        means = [block[:rows, width : width + 1] for block in blocks]
        middle = sum(means) / NX
        spread_ = sum(block[:rows, width + 1 : width + 2] for block in blocks)
        spread_ = spread_ + GW * sum((mean_ - middle) * (mean_ - middle) for mean_ in means)
        inverse = lax.rsqrt(spread_ / (NX * GW) + EPSILON)
        linear = sum(
            block[:rows] + (mean_ - middle) * block[rows : rows + 1]
            for block, mean_ in zip(blocks, means)
        )
        return inverse * linear + sum(block[rows + 1 : rows + 2] for block in blocks)

    own_weight = jnp.where(first, 1.0 - GUIDANCE, GUIDANCE)
    other_weight = jnp.where(first, GUIDANCE, 1.0 - GUIDANCE)
    for d in NEAREST:
        arrived(("own", d))
    guided = own_weight * prediction(0)
    for d in range(NX):
        arrived(("other", d))
    guided = (guided + other_weight * prediction(1)).T
    out_ref[0] = guided[:width]
    for copy in started.values():
        copy.wait_send()


def shards(nz, *args):
    (q, fk, fv, sk, sv, tk, tv, count, positions, shift, scale, proj) = args
    rows, features = q.shape[1], q.shape[2]
    words = tk.shape[1]
    width = proj.shape[1] // 2
    n_copies = len(copy_keys(nz))
    anywhere = pl.BlockSpec(memory_space=pl.ANY)
    in_vmem = pl.BlockSpec(memory_space=pltpu.VMEM)

    def body(*refs):
        kernel(nz, rows, *refs)

    guided = pl.pallas_call(
        body,
        out_shape=jax.ShapeDtypeStruct((1, width, rows), F32),
        in_specs=[anywhere] * 12 + [pl.BlockSpec(memory_space=pltpu.SMEM)],
        out_specs=in_vmem,
        scratch_shapes=[
            pltpu.VMEM((2, rows, features), BF16),
            pltpu.VMEM((NX - 1, rows, GW), BF16),
            pltpu.VMEM((NX - 1, rows, GW), BF16),
            pltpu.VMEM((NX, rows, GW), BF16),
            pltpu.VMEM((NX, rows, GW), BF16),
            pltpu.VMEM((NX, rows, GW), BF16),
            pltpu.VMEM((nz, NC, NX, rows, GW), BF16),
            pltpu.VMEM((nz, NC, NX, rows, GW), BF16),
            pltpu.VMEM((words, GW), BF16),
            pltpu.VMEM((words, GW), BF16),
            pltpu.VMEM((1, GW), F32),
            pltpu.VMEM((1, GW), F32),
            pltpu.VMEM((2 * width, GW), BF16),
            pltpu.VMEM((3, rows), jnp.int32),
            pltpu.VMEM((3, HEAD_DIM), F32),
            pltpu.VMEM((GROUP_HEADS, NX * rows, HEAD_DIM), BF16),
            pltpu.VMEM((GROUP_HEADS, NX * rows, HEAD_DIM), F32),
            pltpu.VMEM((GROUP_HEADS, NX * rows, HEAD_DIM), F32),
            pltpu.VMEM((GROUP_HEADS, NX * rows, HEAD_DIM), F32),
            pltpu.VMEM((2, NX, PACK, HEAD_DIM), F32),
            pltpu.VMEM((2, NX, PACK, HEAD_DIM), F32),
            pltpu.SemaphoreType.DMA((12,)),
            pltpu.SemaphoreType.DMA((n_copies,)),
            pltpu.SemaphoreType.DMA((n_copies,)),
        ],
        compiler_params=pltpu.CompilerParams(
            collective_id=0, has_side_effects=True, vmem_limit_bytes=62 * 1024 * 1024
        ),
        name="stale_attention",
    )(
        q, fk, fv, sk, sv, tk, tv, shift, scale, proj.T, positions, jnp.asarray(lane_frequencies()), count
    )
    return jnp.swapaxes(guided, 1, 2)


def solution(mesh):
    nz = mesh.shape["patch"] // (NX * NC)
    placed = (
        P("cfg", "patch", "rep"),
        P("cfg", "patch", "rep"),
        P("cfg", "patch", "rep"),
        P("cfg", "patch", "rep"),
        P("cfg", "patch", "rep"),
        P("cfg", "rep", None),
        P("cfg", "rep", None),
        P("cfg"),
        P("rep", "patch"),
        P("cfg", None),
        P("cfg", None),
        P(),
    )

    def run(*args):
        return shards(nz, *args)

    return jax.shard_map(
        run, mesh=mesh, in_specs=placed, out_specs=P("cfg", "patch", "rep"), check_vma=False
    )
```

```python
import functools
import math

import jax
import jax.numpy as jnp
import numpy as np
from jax import lax
from jax.experimental import pallas as pl
from jax.experimental.pallas import tpu as pltpu
from jax.sharding import PartitionSpec as P

HEADS = 12
HEAD_DIM = 128
GUIDANCE = 4.0
EPSILON = 1e-06

NX = 4
NC = 2
NEAREST = (1, 3, 2)
GROUP_HEADS = HEADS // NX
GW = GROUP_HEADS * HEAD_DIM
SCALE2 = math.log2(math.e) / math.sqrt(HEAD_DIM)
SIDE = 64
PACK = 16
STEP = 40
F32 = jnp.float32
BF16 = jnp.bfloat16
MESH = pl.DeviceIdType.MESH


def lane_frequencies():
    time_extent = HEAD_DIM // 8
    space_extent = (HEAD_DIM - time_extent) // 2
    rows = np.zeros((3, HEAD_DIM), np.float32)
    start = 0
    for axis, extent in enumerate((time_extent, space_extent, space_extent)):
        exponent = -np.arange(0, extent, 2).astype(np.float32) / np.float32(extent)
        frequency = (256.0 ** exponent.astype(np.float64)).astype(np.float32)
        rows[axis, start : start + extent] = np.repeat(frequency, 2)
        start += extent
    return rows


def turn(value, shift):
    return pltpu.roll(value, shift % HEAD_DIM, 1) if shift % HEAD_DIM else value


def copy_keys(nz):
    keys = [("in", name, d) for name in ("sk", "sv", "q", "fk", "fv") for d in range(1, NX)]
    for kv in ("k", "v"):
        for d in range(NX):
            keys += [("z", kv, 1, d), ("z", kv, nz - 1, d)]
        keys.append(("s", kv, 0))
        for r in range(1, nz):
            keys.append(("s", kv, r))
            if r not in (1, nz - 1):
                keys.append(("z", kv, r))
    keys += [("own", d) for d in range(1, NX)]
    keys += [("other", d) for d in range(NX)]
    return keys


def kernel(
    nz,
    rows,
    q_hbm,
    fk_hbm,
    fv_hbm,
    sk_hbm,
    sv_hbm,
    tk_hbm,
    tv_hbm,
    shift_hbm,
    scale_hbm,
    proj_hbm,
    pos_hbm,
    freq_hbm,
    cnt_ref,
    yrecv,
    raw,
    qsend,
    fksend,
    qbuf,
    fkbuf,
    fvbuf,
    kbuf,
    vbuf,
    tkbuf,
    tvbuf,
    shiftbuf,
    scalebuf,
    projbuf,
    pos_ref,
    freq_ref,
    qh,
    top,
    total,
    acc,
    ysend,
    local_sem,
    send_sem,
    recv_sem,
):
    keys = {key: i for i, key in enumerate(copy_keys(nz))}
    half = nz // 2
    patch = lax.axis_index("patch")
    branch = lax.axis_index("cfg")
    core = lax.rem(patch, NC)
    x = lax.rem(patch // NC, NX)
    z = patch // (NC * NX)

    def at(zz, xx, cc):
        return {"patch": (zz * NX + xx) * NC + cc}

    def owner(d):
        return lax.rem(x + NX - d, NX)

    def asker(d):
        return lax.rem(x + d, NX)

    up = at(lax.rem(z + 1, nz), x, core)
    down = at(lax.rem(z + nz - 1, nz), x, core)
    sibling = at(z, x, 1 - core)

    def across(xx):
        return {"cfg": 1 - branch, **at(z, xx, core)}

    started = {}
    drained = set()

    def send(key, src, dst, device):
        i = keys[key]
        copy = pltpu.make_async_remote_copy(
            src_ref=src,
            dst_ref=dst,
            send_sem=send_sem.at[i],
            recv_sem=recv_sem.at[i],
            device_id=device,
            device_id_type=MESH,
        )
        copy.start()
        started[key] = copy

    def arrived(key):
        started[key].wait_recv()

    def drain(keep=()):
        for key in [key for key in started if key not in drained and key not in keep]:
            started[key].wait_send()
            drained.add(key)

    locals_ = {}

    def fetch(name, src, dst):
        copy = pltpu.make_async_copy(src, dst, local_sem.at[len(locals_)])
        copy.start()
        locals_[name] = copy

    def columns(group):
        return pl.ds(pl.multiple_of(group * GW, 128), GW)

    barrier = pltpu.get_barrier_semaphore()
    friends = [at(z, owner(d), core) for d in range(1, NX)] + [up, down, sibling]
    friends += [across(owner(d)) for d in range(NX)]
    for friend in friends:
        pl.semaphore_signal(barrier, inc=1, device_id=friend, device_id_type=MESH)
    pl.semaphore_wait(barrier, len(friends))

    for name, hbm, buf in (("sk", sk_hbm, kbuf), ("sv", sv_hbm, vbuf)):
        for d in NEAREST:
            send(
                ("in", name, d),
                hbm.at[0, :, columns(owner(d))],
                buf.at[0, 0, d],
                at(z, owner(d), core),
            )

    def spread(kv, src, buf, d):
        send(("z", kv, 1, d), src, buf.at[1, 0, d], up)
        send(("z", kv, nz - 1, d), src, buf.at[nz - 1, 0, d], down)

    spread("k", sk_hbm.at[0, :, columns(x)], kbuf, 0)
    spread("v", sv_hbm.at[0, :, columns(x)], vbuf, 0)

    fetch("pos", pos_hbm, pos_ref)
    fetch("freq", freq_hbm, freq_ref)
    fetch("sk", sk_hbm.at[0, :, columns(x)], kbuf.at[0, 0, 0])
    fetch("sv", sv_hbm.at[0, :, columns(x)], vbuf.at[0, 0, 0])
    fetch("q", q_hbm.at[0], raw.at[0])
    fetch("fk", fk_hbm.at[0], raw.at[1])
    fetch("fv", fv_hbm.at[0, :, columns(x)], fvbuf.at[0])
    fetch("tk", tk_hbm.at[0, :, columns(x)], tkbuf)
    fetch("tv", tv_hbm.at[0, :, columns(x)], tvbuf)
    fetch("shift", shift_hbm.at[:, columns(x)], shiftbuf)
    fetch("scale", scale_hbm.at[:, columns(x)], scalebuf)
    fetch("proj", proj_hbm.at[:, columns(x)], projbuf)

    for name, kv, buf in (("sk", "k", kbuf), ("sv", "v", vbuf)):
        for d in NEAREST:
            arrived(("in", name, d))
            spread(kv, buf.at[0, 0, d], buf, d)
    for kv, buf in (("k", kbuf), ("v", vbuf)):
        locals_["s" + kv].wait()
        send(("s", kv, 0), buf.at[0, 0], buf.at[0, 1], sibling)
    at_row = lax.broadcasted_iota(jnp.int32, (rows, rows), 0)
    at_col = lax.broadcasted_iota(jnp.int32, (rows, rows), 1)
    locals_["pos"].wait()
    locals_["freq"].wait()
    places = pos_ref[...].astype(F32)
    angles = jnp.zeros((rows, HEAD_DIM), F32)
    for axis in range(3):
        column = jnp.sum(
            jnp.where(at_row == at_col, places[axis : axis + 1, :], 0.0), axis=1, keepdims=True
        )
        angles = angles + column * freq_ref[axis : axis + 1, :]
    even = lax.rem(lax.broadcasted_iota(jnp.int32, (rows, HEAD_DIM), 1), 2) == 0
    cosine = jnp.cos(angles)
    sine = jnp.sin(angles)
    sine = jnp.where(even, -sine, sine)
    locals_["q"].wait()
    locals_["fk"].wait()
    for which, name, sendbuf, ownbuf in ((0, "q", qsend, qbuf), (1, "fk", fksend, fkbuf)):
        for d in range(NX):
            for h in range(GROUP_HEADS):
                lanes = pl.ds(pl.multiple_of(owner(d) * GW + h * HEAD_DIM, 128), HEAD_DIM)
                value = raw[which, :, lanes].astype(F32)
                other = jnp.where(
                    even,
                    pltpu.roll(value, HEAD_DIM - 1, 1),
                    pltpu.roll(value, 1, 1),
                )
                turned = (value * cosine + other * sine).astype(BF16)
                target = ownbuf if d == 0 else sendbuf
                target[max(d - 1, 0) if d else 0, :, h * HEAD_DIM : (h + 1) * HEAD_DIM] = turned

    for d in NEAREST:
        send(("in", "q", d), qsend.at[d - 1], qbuf.at[d], at(z, owner(d), core))
    for d in NEAREST:
        send(("in", "fk", d), fksend.at[d - 1], fkbuf.at[d], at(z, owner(d), core))
        send(
            ("in", "fv", d),
            fv_hbm.at[0, :, columns(owner(d))],
            fvbuf.at[d],
            at(z, owner(d), core),
        )

    def lanes_of(h):
        return slice(h * HEAD_DIM, (h + 1) * HEAD_DIM)

    def stacked(buf, h, slots):
        pieces = [
            buf[slot + (d,)][:, lanes_of(h)].astype(F32) for slot in slots for d in range(NX)
        ]
        return jnp.concatenate(pieces, axis=0).astype(BF16)

    def scores_of(h, tile):
        return lax.dot_general(
            qh[h], tile, (((1,), (1,)), ((), ())), preferred_element_type=F32
        )

    def weigh(weights, tile):
        wide = jnp.concatenate([tile, jnp.ones_like(tile)], axis=1)
        return jnp.dot(weights.astype(BF16), wide, preferred_element_type=F32)

    def largest(score):
        return jnp.broadcast_to(
            jnp.max(score, axis=1, keepdims=True), (score.shape[0], HEAD_DIM)
        )

    def relative(score, high):
        copies = -(-score.shape[1] // HEAD_DIM)
        wide = jnp.concatenate([high] * copies, axis=1)[:, : score.shape[1]]
        return jnp.exp2((score - wide) * SCALE2)

    all_rows = NX * rows

    def begin():
        for d in range(1, NX):
            arrived(("in", "q", d))
        for h in range(GROUP_HEADS):
            qh[h] = stacked(qbuf, h, [()])
        for d in range(1, NX):
            arrived(("in", "fk", d))
            arrived(("in", "fv", d))
        locals_["fv"].wait()
        locals_["tk"].wait()
        locals_["tv"].wait()
        block_row = lax.broadcasted_iota(jnp.int32, (all_rows, all_rows), 0) // rows
        block_col = lax.broadcasted_iota(jnp.int32, (all_rows, all_rows), 1) // rows
        same = block_row == block_col
        words = tkbuf.shape[0]
        live = lax.broadcasted_iota(jnp.int32, (all_rows, words), 1) < cnt_ref[0]
        for h in range(GROUP_HEADS):
            own = jnp.where(
                same,
                scores_of(h, stacked(fkbuf, h, [()])),
                scores_of(h, stacked(kbuf, h, [(0, 0)])),
            )
            word = jnp.where(live, scores_of(h, tkbuf[:, lanes_of(h)]), -jnp.inf)
            high = jnp.maximum(largest(own), largest(word))
            own = relative(own, high)
            word = relative(word, high)
            top[h] = high
            summed = (
                weigh(jnp.where(same, own, 0.0), stacked(fvbuf, h, [()]))
                + weigh(jnp.where(same, 0.0, own), stacked(vbuf, h, [(0, 0)]))
                + weigh(word, tvbuf[:, lanes_of(h)])
            )
            acc[h] = summed[:, :HEAD_DIM]
            total[h] = summed[:, HEAD_DIM:]

    def absorbed(h, slots):
        score = scores_of(h, stacked(kbuf, h, slots))
        old = top[h]
        high = jnp.maximum(old, largest(score))
        summed = weigh(relative(score, high), stacked(vbuf, h, slots))
        rescale = jnp.exp2((old - high) * SCALE2)
        return (
            high,
            total[h] * rescale + summed[:, HEAD_DIM:],
            acc[h] * rescale + summed[:, :HEAD_DIM],
        )

    def absorb(slots):
        for h in range(GROUP_HEADS):
            top[h], total[h], acc[h] = absorbed(h, slots)

    def sibling_arrived(r):
        for kv in ("k", "v"):
            arrived(("s", kv, r))

    first = branch == 0
    width = projbuf.shape[0] // 2

    def project(value, tile):
        big = value.astype(BF16)
        small = (value - big.astype(F32)).astype(BF16)
        nt = (((1,), (1,)), ((), ()))
        return lax.dot_general(
            big, tile, nt, preferred_element_type=F32
        ) + lax.dot_general(small, tile, nt, preferred_element_type=F32)

    def forward(kv, buf, t):
        for r, step, device in ((t, 1, up), (nz - t, -1, down)):
            if t == 1:
                for d in range(NX):
                    arrived(("z", kv, r, d))
            else:
                arrived(("z", kv, r))
            following = r + step
            if following != half or (kv == "k") == (step == 1):
                send(("z", kv, following), buf.at[r, 0], buf.at[following, 0], device)
        for r in (t, nz - t):
            send(("s", kv, r), buf.at[r, 0], buf.at[r, 1], sibling)

    both = (("k", kbuf), ("v", vbuf))
    backlog = []
    for t in range(1, half):
        for kv, buf in both:
            forward(kv, buf, t)
            if t == 2 and kv == "k":
                begin()
            elif t >= 2:
                for slot in backlog:
                    if slot[1] == 1:
                        sibling_arrived(slot[0])
                for i in range(0, len(backlog), 4):
                    absorb(backlog[i : i + 4])
                backlog = []
            if kv == "v":
                backlog += [(r, s) for s in (0, 1) for r in (t, nz - t)]
                if t == 1:
                    backlog += [(0, 1)]
    if half == 2:
        begin()
    for name in ("shift", "scale", "proj"):
        locals_[name].wait()
    low, high_half = projbuf[:width], projbuf[width:]
    gap = jnp.zeros((SIDE - width, GW), BF16)
    channels = jnp.concatenate(
        [jnp.where(first, low, high_half), gap, jnp.where(first, high_half, low), gap], axis=0
    )
    gain = 1.0 + scalebuf[...]
    affine = project(
        jnp.concatenate([gain, shiftbuf[...], jnp.zeros((6, GW), F32)], axis=0), channels
    )
    early, late = backlog[:2], backlog[2:]
    absorb(early)
    for slot in late:
        sibling_arrived(slot[0])
    absorb(late)
    drain([("z", "k", half), ("z", "v", half)])
    for kv, buf in both:
        arrived(("z", kv, half))
        send(("s", kv, half), buf.at[half, 0], buf.at[half, 1], sibling)
    absorb([(half, 0)])
    sibling_arrived(half)

    attended = []
    for h in range(GROUP_HEADS):
        _, totals, sums = absorbed(h, [(half, 1)])
        attended.append(sums / totals)
    mean = jnp.sum(sum(attended), axis=1, keepdims=True) / GW
    attended = [part - mean for part in attended]
    squares = jnp.sum(sum(part * part for part in attended), axis=1, keepdims=True)
    share = sum(
        project(attended[h] * gain[:, lanes_of(h)], channels[:, lanes_of(h)])
        for h in range(GROUP_HEADS)
    )
    lane = lax.rem(lax.broadcasted_iota(jnp.int32, share.shape, 1), SIDE)
    share = jnp.where(lane == width, mean, jnp.where(lane == width + 1, squares, share))
    slot = lax.broadcasted_iota(jnp.int32, (PACK, HEAD_DIM), 1) // STEP

    for side, d in [(1, 2), (1, 1), (1, 3), (0, 2), (0, 1), (0, 3), (1, 0), (0, 0)]:
        block = share[d * rows : (d + 1) * rows]
        strips = [
            block[:PACK],
            block[PACK : 2 * PACK],
            jnp.concatenate([block[2 * PACK :], affine], axis=0),
        ]
        strips = [turn(strip, i * STEP - side * SIDE) for i, strip in enumerate(strips)]
        packed = jnp.where(slot == 0, strips[0], jnp.where(slot == 1, strips[1], strips[2]))
        ysend[side, d] = packed
        if (side, d) == (0, 0):
            fetch("self", ysend.at[0, 0], yrecv.at[0, 0])
        else:
            if side:
                send(("other", d), ysend.at[1, d], yrecv.at[1, d], across(asker(d)))
            else:
                send(("own", d), ysend.at[0, d], yrecv.at[0, d], at(z, asker(d), core))

    drain()
    locals_["self"].wait()
    for d in NEAREST:
        arrived(("own", d))
    for d in range(NX):
        arrived(("other", d))


def combine(rows, width, yrecv, out_ref):
    def prediction(side):
        blocks = []
        for d in range(NX):
            packed = yrecv[side, d]
            blocks.append(
                jnp.concatenate([packed, turn(packed, -STEP), turn(packed, -2 * STEP)], axis=0)
            )
        means = [block[:rows, width : width + 1] for block in blocks]
        middle = sum(means) / NX
        spread_ = sum(block[:rows, width + 1 : width + 2] for block in blocks)
        spread_ = spread_ + GW * sum((mean_ - middle) * (mean_ - middle) for mean_ in means)
        inverse = lax.rsqrt(spread_ / (NX * GW) + EPSILON)
        linear = sum(
            block[:rows] + (mean_ - middle) * block[rows : rows + 1]
            for block, mean_ in zip(blocks, means)
        )
        return inverse * linear + sum(block[rows + 1 : rows + 2] for block in blocks)

    first = lax.axis_index("cfg") == 0
    own_weight = jnp.where(first, 1.0 - GUIDANCE, GUIDANCE)
    other_weight = jnp.where(first, GUIDANCE, 1.0 - GUIDANCE)
    guided = (own_weight * prediction(0) + other_weight * prediction(1)).T
    out_ref[0] = guided[:width]


def shards(nz, *args):
    (q, fk, fv, sk, sv, tk, tv, count, positions, shift, scale, proj) = args
    rows, features = q.shape[1], q.shape[2]
    words = tk.shape[1]
    width = proj.shape[1] // 2
    n_copies = len(copy_keys(nz))
    anywhere = pl.BlockSpec(memory_space=pl.ANY)
    in_vmem = pl.BlockSpec(memory_space=pltpu.VMEM)

    def body(*refs):
        kernel(nz, rows, *refs)

    returned = pl.pallas_call(
        body,
        out_shape=jax.ShapeDtypeStruct((2, NX, PACK, HEAD_DIM), F32),
        in_specs=[anywhere] * 12 + [pl.BlockSpec(memory_space=pltpu.SMEM)],
        out_specs=anywhere,
        scratch_shapes=[
            pltpu.VMEM((2, rows, features), BF16),
            pltpu.VMEM((NX - 1, rows, GW), BF16),
            pltpu.VMEM((NX - 1, rows, GW), BF16),
            pltpu.VMEM((NX, rows, GW), BF16),
            pltpu.VMEM((NX, rows, GW), BF16),
            pltpu.VMEM((NX, rows, GW), BF16),
            pltpu.VMEM((nz, NC, NX, rows, GW), BF16),
            pltpu.VMEM((nz, NC, NX, rows, GW), BF16),
            pltpu.VMEM((words, GW), BF16),
            pltpu.VMEM((words, GW), BF16),
            pltpu.VMEM((1, GW), F32),
            pltpu.VMEM((1, GW), F32),
            pltpu.VMEM((2 * width, GW), BF16),
            pltpu.VMEM((3, rows), jnp.int32),
            pltpu.VMEM((3, HEAD_DIM), F32),
            pltpu.VMEM((GROUP_HEADS, NX * rows, HEAD_DIM), BF16),
            pltpu.VMEM((GROUP_HEADS, NX * rows, HEAD_DIM), F32),
            pltpu.VMEM((GROUP_HEADS, NX * rows, HEAD_DIM), F32),
            pltpu.VMEM((GROUP_HEADS, NX * rows, HEAD_DIM), F32),
            pltpu.VMEM((2, NX, PACK, HEAD_DIM), F32),
            pltpu.SemaphoreType.DMA((13,)),
            pltpu.SemaphoreType.DMA((n_copies,)),
            pltpu.SemaphoreType.DMA((n_copies,)),
        ],
        compiler_params=pltpu.CompilerParams(
            collective_id=0, has_side_effects=True, vmem_limit_bytes=62 * 1024 * 1024
        ),
        name="stale_attention",
    )(
        q, fk, fv, sk, sv, tk, tv, shift, scale, proj.T, positions, jnp.asarray(lane_frequencies()), count
    )
    guided = pl.pallas_call(
        functools.partial(combine, rows, width),
        out_shape=jax.ShapeDtypeStruct((1, width, rows), F32),
        in_specs=[in_vmem],
        out_specs=in_vmem,
        name="guided_output",
    )(returned)
    return jnp.swapaxes(guided, 1, 2)


def solution(mesh):
    nz = mesh.shape["patch"] // (NX * NC)
    placed = (
        P("cfg", "patch", "rep"),
        P("cfg", "patch", "rep"),
        P("cfg", "patch", "rep"),
        P("cfg", "patch", "rep"),
        P("cfg", "patch", "rep"),
        P("cfg", "rep", None),
        P("cfg", "rep", None),
        P("cfg"),
        P("rep", "patch"),
        P("cfg", None),
        P("cfg", None),
        P(),
    )

    def run(*args):
        return shards(nz, *args)

    return jax.shard_map(
        run, mesh=mesh, in_specs=placed, out_specs=P("cfg", "patch", "rep"), check_vma=False
    )
```

```python
import functools
import math

import jax
import jax.numpy as jnp
import numpy as np
from jax import lax
from jax.experimental import pallas as pl
from jax.experimental.pallas import tpu as pltpu
from jax.sharding import PartitionSpec as P

HEADS = 12
HEAD_DIM = 128
GUIDANCE = 4.0
EPSILON = 1e-06

NX = 4
NC = 2
NEAREST = (1, 3, 2)
GROUP_HEADS = HEADS // NX
GW = GROUP_HEADS * HEAD_DIM
SCALE2 = math.log2(math.e) / math.sqrt(HEAD_DIM)
SIDE = 64
PACK = 16
STEP = 40
F32 = jnp.float32
BF16 = jnp.bfloat16
MESH = pl.DeviceIdType.MESH


def lane_frequencies():
    time_extent = HEAD_DIM // 8
    space_extent = (HEAD_DIM - time_extent) // 2
    rows = np.zeros((3, HEAD_DIM), np.float32)
    start = 0
    for axis, extent in enumerate((time_extent, space_extent, space_extent)):
        exponent = -np.arange(0, extent, 2).astype(np.float32) / np.float32(extent)
        frequency = (256.0 ** exponent.astype(np.float64)).astype(np.float32)
        rows[axis, start : start + extent] = np.repeat(frequency, 2)
        start += extent
    return rows


def turn(value, shift):
    return pltpu.roll(value, shift % HEAD_DIM, 1) if shift % HEAD_DIM else value


def copy_keys(nz):
    keys = [("in", name, d) for name in ("sk", "sv", "q", "fk", "fv") for d in range(1, NX)]
    for kv in ("k", "v"):
        for d in range(NX):
            keys += [("z", kv, 1, d), ("z", kv, nz - 1, d)]
        keys.append(("s", kv, 0))
        for r in range(1, nz):
            keys.append(("s", kv, r))
            if r not in (1, nz - 1):
                keys.append(("z", kv, r))
    keys += [("own", d) for d in range(1, NX)]
    keys += [("other", d) for d in range(NX)]
    return keys


def kernel(
    nz,
    rows,
    q_hbm,
    fk_hbm,
    fv_hbm,
    sk_hbm,
    sv_hbm,
    tk_hbm,
    tv_hbm,
    shift_hbm,
    scale_hbm,
    proj_hbm,
    pos_hbm,
    freq_hbm,
    cnt_ref,
    yrecv,
    raw,
    qsend,
    fksend,
    qbuf,
    fkbuf,
    fvbuf,
    kbuf,
    vbuf,
    tkbuf,
    tvbuf,
    shiftbuf,
    scalebuf,
    projbuf,
    pos_ref,
    freq_ref,
    qh,
    top,
    total,
    acc,
    ysend,
    local_sem,
    send_sem,
    recv_sem,
):
    keys = {key: i for i, key in enumerate(copy_keys(nz))}
    half = nz // 2
    patch = lax.axis_index("patch")
    branch = lax.axis_index("cfg")
    core = lax.rem(patch, NC)
    x = lax.rem(patch // NC, NX)
    z = patch // (NC * NX)

    def at(zz, xx, cc):
        return {"patch": (zz * NX + xx) * NC + cc}

    def owner(d):
        return lax.rem(x + NX - d, NX)

    def asker(d):
        return lax.rem(x + d, NX)

    up = at(lax.rem(z + 1, nz), x, core)
    down = at(lax.rem(z + nz - 1, nz), x, core)
    sibling = at(z, x, 1 - core)

    def across(xx):
        return {"cfg": 1 - branch, **at(z, xx, core)}

    started = {}
    drained = set()

    def send(key, src, dst, device):
        i = keys[key]
        copy = pltpu.make_async_remote_copy(
            src_ref=src,
            dst_ref=dst,
            send_sem=send_sem.at[i],
            recv_sem=recv_sem.at[i],
            device_id=device,
            device_id_type=MESH,
        )
        copy.start()
        started[key] = copy

    def arrived(key):
        started[key].wait_recv()

    def drain(keep=()):
        for key in [key for key in started if key not in drained and key not in keep]:
            started[key].wait_send()
            drained.add(key)

    locals_ = {}

    def fetch(name, src, dst):
        copy = pltpu.make_async_copy(src, dst, local_sem.at[len(locals_)])
        copy.start()
        locals_[name] = copy

    def columns(group):
        return pl.ds(pl.multiple_of(group * GW, 128), GW)

    barrier = pltpu.get_barrier_semaphore()
    friends = [at(z, owner(d), core) for d in range(1, NX)] + [up, down, sibling]
    friends += [across(x)]
    for friend in friends:
        pl.semaphore_signal(barrier, inc=1, device_id=friend, device_id_type=MESH)
    pl.semaphore_wait(barrier, len(friends))

    for name, hbm, buf in (("sk", sk_hbm, kbuf), ("sv", sv_hbm, vbuf)):
        for d in NEAREST:
            send(
                ("in", name, d),
                hbm.at[0, :, columns(owner(d))],
                buf.at[0, 0, d],
                at(z, owner(d), core),
            )

    def spread(kv, src, buf, d):
        send(("z", kv, 1, d), src, buf.at[1, 0, d], up)
        send(("z", kv, nz - 1, d), src, buf.at[nz - 1, 0, d], down)

    spread("k", sk_hbm.at[0, :, columns(x)], kbuf, 0)
    spread("v", sv_hbm.at[0, :, columns(x)], vbuf, 0)

    fetch("pos", pos_hbm, pos_ref)
    fetch("freq", freq_hbm, freq_ref)
    fetch("sk", sk_hbm.at[0, :, columns(x)], kbuf.at[0, 0, 0])
    fetch("sv", sv_hbm.at[0, :, columns(x)], vbuf.at[0, 0, 0])
    fetch("q", q_hbm.at[0], raw.at[0])
    fetch("fk", fk_hbm.at[0], raw.at[1])
    fetch("fv", fv_hbm.at[0, :, columns(x)], fvbuf.at[0])
    fetch("tk", tk_hbm.at[0, :, columns(x)], tkbuf)
    fetch("tv", tv_hbm.at[0, :, columns(x)], tvbuf)
    fetch("shift", shift_hbm.at[:, columns(x)], shiftbuf)
    fetch("scale", scale_hbm.at[:, columns(x)], scalebuf)
    fetch("proj", proj_hbm.at[:, columns(x)], projbuf)

    for name, kv, buf in (("sk", "k", kbuf), ("sv", "v", vbuf)):
        for d in NEAREST:
            arrived(("in", name, d))
            spread(kv, buf.at[0, 0, d], buf, d)
    for kv, buf in (("k", kbuf), ("v", vbuf)):
        locals_["s" + kv].wait()
        send(("s", kv, 0), buf.at[0, 0], buf.at[0, 1], sibling)
    at_row = lax.broadcasted_iota(jnp.int32, (rows, rows), 0)
    at_col = lax.broadcasted_iota(jnp.int32, (rows, rows), 1)
    locals_["pos"].wait()
    locals_["freq"].wait()
    places = pos_ref[...].astype(F32)
    angles = jnp.zeros((rows, HEAD_DIM), F32)
    for axis in range(3):
        column = jnp.sum(
            jnp.where(at_row == at_col, places[axis : axis + 1, :], 0.0), axis=1, keepdims=True
        )
        angles = angles + column * freq_ref[axis : axis + 1, :]
    even = lax.rem(lax.broadcasted_iota(jnp.int32, (rows, HEAD_DIM), 1), 2) == 0
    cosine = jnp.cos(angles)
    sine = jnp.sin(angles)
    sine = jnp.where(even, -sine, sine)
    locals_["q"].wait()
    locals_["fk"].wait()
    for which, name, sendbuf, ownbuf in ((0, "q", qsend, qbuf), (1, "fk", fksend, fkbuf)):
        for d in range(NX):
            for h in range(GROUP_HEADS):
                lanes = pl.ds(pl.multiple_of(owner(d) * GW + h * HEAD_DIM, 128), HEAD_DIM)
                value = raw[which, :, lanes].astype(F32)
                other = jnp.where(
                    even,
                    pltpu.roll(value, HEAD_DIM - 1, 1),
                    pltpu.roll(value, 1, 1),
                )
                turned = (value * cosine + other * sine).astype(BF16)
                target = ownbuf if d == 0 else sendbuf
                target[max(d - 1, 0) if d else 0, :, h * HEAD_DIM : (h + 1) * HEAD_DIM] = turned

    for d in NEAREST:
        send(("in", "q", d), qsend.at[d - 1], qbuf.at[d], at(z, owner(d), core))
    for d in NEAREST:
        send(("in", "fk", d), fksend.at[d - 1], fkbuf.at[d], at(z, owner(d), core))
        send(
            ("in", "fv", d),
            fv_hbm.at[0, :, columns(owner(d))],
            fvbuf.at[d],
            at(z, owner(d), core),
        )

    def lanes_of(h):
        return slice(h * HEAD_DIM, (h + 1) * HEAD_DIM)

    def stacked(buf, h, slots):
        pieces = [
            buf[slot + (d,)][:, lanes_of(h)].astype(F32) for slot in slots for d in range(NX)
        ]
        return jnp.concatenate(pieces, axis=0).astype(BF16)

    def scores_of(h, tile):
        return lax.dot_general(
            qh[h], tile, (((1,), (1,)), ((), ())), preferred_element_type=F32
        )

    def weigh(weights, tile):
        wide = jnp.concatenate([tile, jnp.ones_like(tile)], axis=1)
        return jnp.dot(weights.astype(BF16), wide, preferred_element_type=F32)

    def largest(score):
        return jnp.broadcast_to(
            jnp.max(score, axis=1, keepdims=True), (score.shape[0], HEAD_DIM)
        )

    def relative(score, high):
        copies = -(-score.shape[1] // HEAD_DIM)
        wide = jnp.concatenate([high] * copies, axis=1)[:, : score.shape[1]]
        return jnp.exp2((score - wide) * SCALE2)

    all_rows = NX * rows

    def begin():
        for d in range(1, NX):
            arrived(("in", "q", d))
        for h in range(GROUP_HEADS):
            qh[h] = stacked(qbuf, h, [()])
        for d in range(1, NX):
            arrived(("in", "fk", d))
            arrived(("in", "fv", d))
        locals_["fv"].wait()
        locals_["tk"].wait()
        locals_["tv"].wait()
        block_row = lax.broadcasted_iota(jnp.int32, (all_rows, all_rows), 0) // rows
        block_col = lax.broadcasted_iota(jnp.int32, (all_rows, all_rows), 1) // rows
        same = block_row == block_col
        words = tkbuf.shape[0]
        live = lax.broadcasted_iota(jnp.int32, (all_rows, words), 1) < cnt_ref[0]
        for h in range(GROUP_HEADS):
            own = jnp.where(
                same,
                scores_of(h, stacked(fkbuf, h, [()])),
                scores_of(h, stacked(kbuf, h, [(0, 0)])),
            )
            word = jnp.where(live, scores_of(h, tkbuf[:, lanes_of(h)]), -jnp.inf)
            high = jnp.maximum(largest(own), largest(word))
            own = relative(own, high)
            word = relative(word, high)
            top[h] = high
            summed = (
                weigh(jnp.where(same, own, 0.0), stacked(fvbuf, h, [()]))
                + weigh(jnp.where(same, 0.0, own), stacked(vbuf, h, [(0, 0)]))
                + weigh(word, tvbuf[:, lanes_of(h)])
            )
            acc[h] = summed[:, :HEAD_DIM]
            total[h] = summed[:, HEAD_DIM:]

    def absorbed(h, slots):
        score = scores_of(h, stacked(kbuf, h, slots))
        old = top[h]
        high = jnp.maximum(old, largest(score))
        summed = weigh(relative(score, high), stacked(vbuf, h, slots))
        rescale = jnp.exp2((old - high) * SCALE2)
        return (
            high,
            total[h] * rescale + summed[:, HEAD_DIM:],
            acc[h] * rescale + summed[:, :HEAD_DIM],
        )

    def absorb(slots):
        for h in range(GROUP_HEADS):
            top[h], total[h], acc[h] = absorbed(h, slots)

    def sibling_arrived(r):
        for kv in ("k", "v"):
            arrived(("s", kv, r))

    first = branch == 0
    width = projbuf.shape[0] // 2

    def project(value, tile):
        big = value.astype(BF16)
        small = (value - big.astype(F32)).astype(BF16)
        nt = (((1,), (1,)), ((), ()))
        return lax.dot_general(
            big, tile, nt, preferred_element_type=F32
        ) + lax.dot_general(small, tile, nt, preferred_element_type=F32)

    def forward(kv, buf, t):
        for r, step, device in ((t, 1, up), (nz - t, -1, down)):
            if t == 1:
                for d in range(NX):
                    arrived(("z", kv, r, d))
            else:
                arrived(("z", kv, r))
            following = r + step
            if following != half or (kv == "k") == (step == 1):
                send(("z", kv, following), buf.at[r, 0], buf.at[following, 0], device)
        for r in (t, nz - t):
            send(("s", kv, r), buf.at[r, 0], buf.at[r, 1], sibling)

    both = (("k", kbuf), ("v", vbuf))
    backlog = []
    for t in range(1, half):
        for kv, buf in both:
            forward(kv, buf, t)
            if t == 2 and kv == "k":
                begin()
            elif t >= 2:
                for slot in backlog:
                    if slot[1] == 1:
                        sibling_arrived(slot[0])
                for i in range(0, len(backlog), 4):
                    absorb(backlog[i : i + 4])
                backlog = []
            if kv == "v":
                backlog += [(r, s) for s in (0, 1) for r in (t, nz - t)]
                if t == 1:
                    backlog += [(0, 1)]
    if half == 2:
        begin()
    for name in ("shift", "scale", "proj"):
        locals_[name].wait()
    low, high_half = projbuf[:width], projbuf[width:]
    gap = jnp.zeros((SIDE - width, GW), BF16)
    channels = jnp.concatenate(
        [jnp.where(first, low, high_half), gap, jnp.where(first, high_half, low), gap], axis=0
    )
    gain = 1.0 + scalebuf[...]
    affine = project(
        jnp.concatenate([gain, shiftbuf[...], jnp.zeros((6, GW), F32)], axis=0), channels
    )
    early, late = backlog[:2], backlog[2:]
    absorb(early)
    for slot in late:
        sibling_arrived(slot[0])
    absorb(late)
    drain([("z", "k", half), ("z", "v", half)])
    for kv, buf in both:
        arrived(("z", kv, half))
        send(("s", kv, half), buf.at[half, 0], buf.at[half, 1], sibling)
    absorb([(half, 0)])
    sibling_arrived(half)

    attended = []
    for h in range(GROUP_HEADS):
        _, totals, sums = absorbed(h, [(half, 1)])
        attended.append(sums / totals)
    mean = jnp.sum(sum(attended), axis=1, keepdims=True) / GW
    attended = [part - mean for part in attended]
    squares = jnp.sum(sum(part * part for part in attended), axis=1, keepdims=True)
    share = sum(
        project(attended[h] * gain[:, lanes_of(h)], channels[:, lanes_of(h)])
        for h in range(GROUP_HEADS)
    )
    lane = lax.rem(lax.broadcasted_iota(jnp.int32, share.shape, 1), SIDE)
    share = jnp.where(lane == width, mean, jnp.where(lane == width + 1, squares, share))
    slot = lax.broadcasted_iota(jnp.int32, (PACK, HEAD_DIM), 1) // STEP

    for side, d in [(1, 2), (1, 1), (1, 3), (0, 2), (0, 1), (0, 3), (1, 0), (0, 0)]:
        block = share[d * rows : (d + 1) * rows]
        strips = [
            block[:PACK],
            block[PACK : 2 * PACK],
            jnp.concatenate([block[2 * PACK :], affine], axis=0),
        ]
        strips = [turn(strip, i * STEP - side * SIDE) for i, strip in enumerate(strips)]
        packed = jnp.where(slot == 0, strips[0], jnp.where(slot == 1, strips[1], strips[2]))
        ysend[side, d] = packed
        if (side, d) == (0, 0):
            fetch("self", ysend.at[0, 0], yrecv.at[0, 0])
        else:
            if side:
                send(("other", d), ysend.at[1, d], yrecv.at[1, d], across(asker(d)))
            else:
                send(("own", d), ysend.at[0, d], yrecv.at[0, d], at(z, asker(d), core))

    drain()
    locals_["self"].wait()
    for d in NEAREST:
        arrived(("own", d))
    for d in range(NX):
        arrived(("other", d))


def combine(rows, width, yrecv, out_ref):
    def prediction(side):
        blocks = []
        for d in range(NX):
            packed = yrecv[side, d]
            blocks.append(
                jnp.concatenate([packed, turn(packed, -STEP), turn(packed, -2 * STEP)], axis=0)
            )
        means = [block[:rows, width : width + 1] for block in blocks]
        middle = sum(means) / NX
        spread_ = sum(block[:rows, width + 1 : width + 2] for block in blocks)
        spread_ = spread_ + GW * sum((mean_ - middle) * (mean_ - middle) for mean_ in means)
        inverse = lax.rsqrt(spread_ / (NX * GW) + EPSILON)
        linear = sum(
            block[:rows] + (mean_ - middle) * block[rows : rows + 1]
            for block, mean_ in zip(blocks, means)
        )
        return inverse * linear + sum(block[rows + 1 : rows + 2] for block in blocks)

    first = lax.axis_index("cfg") == 0
    own_weight = jnp.where(first, 1.0 - GUIDANCE, GUIDANCE)
    other_weight = jnp.where(first, GUIDANCE, 1.0 - GUIDANCE)
    guided = (own_weight * prediction(0) + other_weight * prediction(1)).T
    out_ref[0] = guided[:width]


def shards(nz, *args):
    (q, fk, fv, sk, sv, tk, tv, count, positions, shift, scale, proj) = args
    rows, features = q.shape[1], q.shape[2]
    words = tk.shape[1]
    width = proj.shape[1] // 2
    n_copies = len(copy_keys(nz))
    anywhere = pl.BlockSpec(memory_space=pl.ANY)
    in_vmem = pl.BlockSpec(memory_space=pltpu.VMEM)

    def body(*refs):
        kernel(nz, rows, *refs)

    returned = pl.pallas_call(
        body,
        out_shape=jax.ShapeDtypeStruct((2, NX, PACK, HEAD_DIM), F32),
        in_specs=[anywhere] * 12 + [pl.BlockSpec(memory_space=pltpu.SMEM)],
        out_specs=anywhere,
        scratch_shapes=[
            pltpu.VMEM((2, rows, features), BF16),
            pltpu.VMEM((NX - 1, rows, GW), BF16),
            pltpu.VMEM((NX - 1, rows, GW), BF16),
            pltpu.VMEM((NX, rows, GW), BF16),
            pltpu.VMEM((NX, rows, GW), BF16),
            pltpu.VMEM((NX, rows, GW), BF16),
            pltpu.VMEM((nz, NC, NX, rows, GW), BF16),
            pltpu.VMEM((nz, NC, NX, rows, GW), BF16),
            pltpu.VMEM((words, GW), BF16),
            pltpu.VMEM((words, GW), BF16),
            pltpu.VMEM((1, GW), F32),
            pltpu.VMEM((1, GW), F32),
            pltpu.VMEM((2 * width, GW), BF16),
            pltpu.VMEM((3, rows), jnp.int32),
            pltpu.VMEM((3, HEAD_DIM), F32),
            pltpu.VMEM((GROUP_HEADS, NX * rows, HEAD_DIM), BF16),
            pltpu.VMEM((GROUP_HEADS, NX * rows, HEAD_DIM), F32),
            pltpu.VMEM((GROUP_HEADS, NX * rows, HEAD_DIM), F32),
            pltpu.VMEM((GROUP_HEADS, NX * rows, HEAD_DIM), F32),
            pltpu.VMEM((2, NX, PACK, HEAD_DIM), F32),
            pltpu.SemaphoreType.DMA((13,)),
            pltpu.SemaphoreType.DMA((n_copies,)),
            pltpu.SemaphoreType.DMA((n_copies,)),
        ],
        compiler_params=pltpu.CompilerParams(
            collective_id=0, has_side_effects=True, vmem_limit_bytes=62 * 1024 * 1024
        ),
        name="stale_attention",
    )(
        q, fk, fv, sk, sv, tk, tv, shift, scale, proj.T, positions, jnp.asarray(lane_frequencies()), count
    )
    guided = pl.pallas_call(
        functools.partial(combine, rows, width),
        out_shape=jax.ShapeDtypeStruct((1, width, rows), F32),
        in_specs=[in_vmem],
        out_specs=in_vmem,
        name="guided_output",
    )(returned)
    return jnp.swapaxes(guided, 1, 2)


def solution(mesh):
    nz = mesh.shape["patch"] // (NX * NC)
    placed = (
        P("cfg", "patch", "rep"),
        P("cfg", "patch", "rep"),
        P("cfg", "patch", "rep"),
        P("cfg", "patch", "rep"),
        P("cfg", "patch", "rep"),
        P("cfg", "rep", None),
        P("cfg", "rep", None),
        P("cfg"),
        P("rep", "patch"),
        P("cfg", None),
        P("cfg", None),
        P(),
    )

    def run(*args):
        return shards(nz, *args)

    return jax.shard_map(
        run, mesh=mesh, in_specs=placed, out_specs=P("cfg", "patch", "rep"), check_vma=False
    )
```

```python
import functools
import math

import jax
import jax.numpy as jnp
import numpy as np
from jax import lax
from jax.experimental import pallas as pl
from jax.experimental.pallas import tpu as pltpu
from jax.sharding import PartitionSpec as P

HEADS = 12
HEAD_DIM = 128
GUIDANCE = 4.0
EPSILON = 1e-06

NX = 4
NC = 2
NEAREST = (1, 3, 2)
GROUP_HEADS = HEADS // NX
GW = GROUP_HEADS * HEAD_DIM
SCALE2 = math.log2(math.e) / math.sqrt(HEAD_DIM)
SIDE = 64
PACK = 16
STEP = 40
F32 = jnp.float32
BF16 = jnp.bfloat16
MESH = pl.DeviceIdType.MESH


def lane_frequencies():
    time_extent = HEAD_DIM // 8
    space_extent = (HEAD_DIM - time_extent) // 2
    rows = np.zeros((3, HEAD_DIM), np.float32)
    start = 0
    for axis, extent in enumerate((time_extent, space_extent, space_extent)):
        exponent = -np.arange(0, extent, 2).astype(np.float32) / np.float32(extent)
        frequency = (256.0 ** exponent.astype(np.float64)).astype(np.float32)
        rows[axis, start : start + extent] = np.repeat(frequency, 2)
        start += extent
    return rows


def turn(value, shift):
    return pltpu.roll(value, shift % HEAD_DIM, 1) if shift % HEAD_DIM else value


def copy_keys(nz):
    keys = [("in", name, d) for name in ("sk", "sv", "q", "fk", "fv") for d in range(1, NX)]
    for kv in ("k", "v"):
        for d in range(NX):
            keys += [("z", kv, 1, d), ("z", kv, nz - 1, d)]
        keys.append(("s", kv, 0))
        for r in range(1, nz):
            if r == nz // 2:
                keys += [(way, kv, r, part) for way in ("s", "z") for part in (0, 1)]
                continue
            keys.append(("s", kv, r))
            if r not in (1, nz - 1):
                keys.append(("z", kv, r))
    keys += [("own", d) for d in range(1, NX)]
    keys += [("other", d) for d in range(NX)]
    return keys


def kernel(
    nz,
    rows,
    q_hbm,
    fk_hbm,
    fv_hbm,
    sk_hbm,
    sv_hbm,
    tk_hbm,
    tv_hbm,
    shift_hbm,
    scale_hbm,
    proj_hbm,
    pos_hbm,
    freq_hbm,
    cnt_ref,
    yrecv,
    raw,
    qsend,
    fksend,
    qbuf,
    fkbuf,
    fvbuf,
    kbuf,
    vbuf,
    tkbuf,
    tvbuf,
    shiftbuf,
    scalebuf,
    projbuf,
    pos_ref,
    freq_ref,
    qh,
    top,
    total,
    acc,
    ysend,
    local_sem,
    send_sem,
    recv_sem,
):
    keys = {key: i for i, key in enumerate(copy_keys(nz))}
    half = nz // 2
    patch = lax.axis_index("patch")
    branch = lax.axis_index("cfg")
    core = lax.rem(patch, NC)
    x = lax.rem(patch // NC, NX)
    z = patch // (NC * NX)

    def at(zz, xx, cc):
        return {"patch": (zz * NX + xx) * NC + cc}

    def owner(d):
        return lax.rem(x + NX - d, NX)

    def asker(d):
        return lax.rem(x + d, NX)

    up = at(lax.rem(z + 1, nz), x, core)
    down = at(lax.rem(z + nz - 1, nz), x, core)
    sibling = at(z, x, 1 - core)

    def across(xx):
        return {"cfg": 1 - branch, **at(z, xx, core)}

    started = {}
    drained = set()

    def send(key, src, dst, device):
        i = keys[key]
        copy = pltpu.make_async_remote_copy(
            src_ref=src,
            dst_ref=dst,
            send_sem=send_sem.at[i],
            recv_sem=recv_sem.at[i],
            device_id=device,
            device_id_type=MESH,
        )
        copy.start()
        started[key] = copy

    def arrived(key):
        started[key].wait_recv()

    def drain(keep=()):
        for key in [key for key in started if key not in drained and key not in keep]:
            started[key].wait_send()
            drained.add(key)

    locals_ = {}

    def fetch(name, src, dst):
        copy = pltpu.make_async_copy(src, dst, local_sem.at[len(locals_)])
        copy.start()
        locals_[name] = copy

    def columns(group):
        return pl.ds(pl.multiple_of(group * GW, 128), GW)

    barrier = pltpu.get_barrier_semaphore()
    friends = [at(z, owner(d), core) for d in range(1, NX)] + [up, down, sibling]
    friends += [across(x)]
    for friend in friends:
        pl.semaphore_signal(barrier, inc=1, device_id=friend, device_id_type=MESH)
    pl.semaphore_wait(barrier, len(friends))

    for name, hbm, buf in (("sk", sk_hbm, kbuf), ("sv", sv_hbm, vbuf)):
        for d in NEAREST:
            send(
                ("in", name, d),
                hbm.at[0, :, columns(owner(d))],
                buf.at[0, 0, d],
                at(z, owner(d), core),
            )

    def spread(kv, src, buf, d):
        send(("z", kv, 1, d), src, buf.at[1, 0, d], up)
        send(("z", kv, nz - 1, d), src, buf.at[nz - 1, 0, d], down)

    spread("k", sk_hbm.at[0, :, columns(x)], kbuf, 0)
    spread("v", sv_hbm.at[0, :, columns(x)], vbuf, 0)

    fetch("pos", pos_hbm, pos_ref)
    fetch("freq", freq_hbm, freq_ref)
    fetch("sk", sk_hbm.at[0, :, columns(x)], kbuf.at[0, 0, 0])
    fetch("sv", sv_hbm.at[0, :, columns(x)], vbuf.at[0, 0, 0])
    fetch("q", q_hbm.at[0], raw.at[0])
    fetch("fk", fk_hbm.at[0], raw.at[1])
    fetch("fv", fv_hbm.at[0, :, columns(x)], fvbuf.at[0])
    fetch("tk", tk_hbm.at[0, :, columns(x)], tkbuf)
    fetch("tv", tv_hbm.at[0, :, columns(x)], tvbuf)
    fetch("shift", shift_hbm.at[:, columns(x)], shiftbuf)
    fetch("scale", scale_hbm.at[:, columns(x)], scalebuf)
    fetch("proj", proj_hbm.at[:, columns(x)], projbuf)

    for name, kv, buf in (("sk", "k", kbuf), ("sv", "v", vbuf)):
        for d in NEAREST:
            arrived(("in", name, d))
            spread(kv, buf.at[0, 0, d], buf, d)
    for kv, buf in (("k", kbuf), ("v", vbuf)):
        locals_["s" + kv].wait()
        send(("s", kv, 0), buf.at[0, 0], buf.at[0, 1], sibling)
    at_row = lax.broadcasted_iota(jnp.int32, (rows, rows), 0)
    at_col = lax.broadcasted_iota(jnp.int32, (rows, rows), 1)
    locals_["pos"].wait()
    locals_["freq"].wait()
    places = pos_ref[...].astype(F32)
    angles = jnp.zeros((rows, HEAD_DIM), F32)
    for axis in range(3):
        column = jnp.sum(
            jnp.where(at_row == at_col, places[axis : axis + 1, :], 0.0), axis=1, keepdims=True
        )
        angles = angles + column * freq_ref[axis : axis + 1, :]
    even = lax.rem(lax.broadcasted_iota(jnp.int32, (rows, HEAD_DIM), 1), 2) == 0
    cosine = jnp.cos(angles)
    sine = jnp.sin(angles)
    sine = jnp.where(even, -sine, sine)
    locals_["q"].wait()
    locals_["fk"].wait()
    for which, name, sendbuf, ownbuf in ((0, "q", qsend, qbuf), (1, "fk", fksend, fkbuf)):
        for d in range(NX):
            for h in range(GROUP_HEADS):
                lanes = pl.ds(pl.multiple_of(owner(d) * GW + h * HEAD_DIM, 128), HEAD_DIM)
                value = raw[which, :, lanes].astype(F32)
                other = jnp.where(
                    even,
                    pltpu.roll(value, HEAD_DIM - 1, 1),
                    pltpu.roll(value, 1, 1),
                )
                turned = (value * cosine + other * sine).astype(BF16)
                target = ownbuf if d == 0 else sendbuf
                target[max(d - 1, 0) if d else 0, :, h * HEAD_DIM : (h + 1) * HEAD_DIM] = turned

    for d in NEAREST:
        send(("in", "q", d), qsend.at[d - 1], qbuf.at[d], at(z, owner(d), core))
    for d in NEAREST:
        send(("in", "fk", d), fksend.at[d - 1], fkbuf.at[d], at(z, owner(d), core))
        send(
            ("in", "fv", d),
            fv_hbm.at[0, :, columns(owner(d))],
            fvbuf.at[d],
            at(z, owner(d), core),
        )

    def lanes_of(h):
        return slice(h * HEAD_DIM, (h + 1) * HEAD_DIM)

    def stacked(buf, h, slots):
        pieces = [
            buf[slot + (d,)][:, lanes_of(h)].astype(F32) for slot in slots for d in range(NX)
        ]
        return jnp.concatenate(pieces, axis=0).astype(BF16)

    def scores_of(h, tile):
        return lax.dot_general(
            qh[h], tile, (((1,), (1,)), ((), ())), preferred_element_type=F32
        )

    def weigh(weights, tile):
        wide = jnp.concatenate([tile, jnp.ones_like(tile)], axis=1)
        return jnp.dot(weights.astype(BF16), wide, preferred_element_type=F32)

    def largest(score):
        return jnp.broadcast_to(
            jnp.max(score, axis=1, keepdims=True), (score.shape[0], HEAD_DIM)
        )

    def relative(score, high):
        copies = -(-score.shape[1] // HEAD_DIM)
        wide = jnp.concatenate([high] * copies, axis=1)[:, : score.shape[1]]
        return jnp.exp2((score - wide) * SCALE2)

    all_rows = NX * rows

    def begin():
        for d in range(1, NX):
            arrived(("in", "q", d))
        for h in range(GROUP_HEADS):
            qh[h] = stacked(qbuf, h, [()])
        for d in range(1, NX):
            arrived(("in", "fk", d))
            arrived(("in", "fv", d))
        locals_["fv"].wait()
        locals_["tk"].wait()
        locals_["tv"].wait()
        block_row = lax.broadcasted_iota(jnp.int32, (all_rows, all_rows), 0) // rows
        block_col = lax.broadcasted_iota(jnp.int32, (all_rows, all_rows), 1) // rows
        same = block_row == block_col
        words = tkbuf.shape[0]
        live = lax.broadcasted_iota(jnp.int32, (all_rows, words), 1) < cnt_ref[0]
        for h in range(GROUP_HEADS):
            own = jnp.where(
                same,
                scores_of(h, stacked(fkbuf, h, [()])),
                scores_of(h, stacked(kbuf, h, [(0, 0)])),
            )
            word = jnp.where(live, scores_of(h, tkbuf[:, lanes_of(h)]), -jnp.inf)
            high = jnp.maximum(largest(own), largest(word))
            own = relative(own, high)
            word = relative(word, high)
            top[h] = high
            summed = (
                weigh(jnp.where(same, own, 0.0), stacked(fvbuf, h, [()]))
                + weigh(jnp.where(same, 0.0, own), stacked(vbuf, h, [(0, 0)]))
                + weigh(word, tvbuf[:, lanes_of(h)])
            )
            acc[h] = summed[:, :HEAD_DIM]
            total[h] = summed[:, HEAD_DIM:]

    def absorbed(h, slots):
        score = scores_of(h, stacked(kbuf, h, slots))
        old = top[h]
        high = jnp.maximum(old, largest(score))
        summed = weigh(relative(score, high), stacked(vbuf, h, slots))
        rescale = jnp.exp2((old - high) * SCALE2)
        return (
            high,
            total[h] * rescale + summed[:, HEAD_DIM:],
            acc[h] * rescale + summed[:, :HEAD_DIM],
        )

    def absorb(slots):
        for h in range(GROUP_HEADS):
            top[h], total[h], acc[h] = absorbed(h, slots)

    def sibling_arrived(r):
        for kv in ("k", "v"):
            arrived(("s", kv, r))

    first = branch == 0
    width = projbuf.shape[0] // 2

    def project(value, tile):
        big = value.astype(BF16)
        small = (value - big.astype(F32)).astype(BF16)
        nt = (((1,), (1,)), ((), ()))
        return lax.dot_general(
            big, tile, nt, preferred_element_type=F32
        ) + lax.dot_general(small, tile, nt, preferred_element_type=F32)

    def forward(kv, buf, t):
        for r, step, device in ((t, 1, up), (nz - t, -1, down)):
            if t == 1:
                for d in range(NX):
                    arrived(("z", kv, r, d))
            else:
                arrived(("z", kv, r))
            following = r + step
            if following != half:
                send(("z", kv, following), buf.at[r, 0], buf.at[following, 0], device)
            elif (kv == "k") == (step == 1):
                for part in (0, 1):
                    some = pl.ds(part * NX // 2, NX // 2)
                    source, target = buf.at[r, 0, some], buf.at[half, 0, some]
                    send(("z", kv, half, part), source, target, device)
        for r in (t, nz - t):
            send(("s", kv, r), buf.at[r, 0], buf.at[r, 1], sibling)

    both = (("k", kbuf), ("v", vbuf))
    backlog = []
    for t in range(1, half):
        for kv, buf in both:
            forward(kv, buf, t)
            if t == 2 and kv == "k":
                begin()
            elif t >= 2:
                for slot in backlog:
                    if slot[1] == 1:
                        sibling_arrived(slot[0])
                for i in range(0, len(backlog), 4):
                    absorb(backlog[i : i + 4])
                backlog = []
            if kv == "v":
                backlog += [(r, s) for s in (0, 1) for r in (t, nz - t)]
                if t == 1:
                    backlog += [(0, 1)]
    if half == 2:
        begin()
    for name in ("shift", "scale", "proj"):
        locals_[name].wait()
    low, high_half = projbuf[:width], projbuf[width:]
    gap = jnp.zeros((SIDE - width, GW), BF16)
    channels = jnp.concatenate(
        [jnp.where(first, low, high_half), gap, jnp.where(first, high_half, low), gap], axis=0
    )
    gain = 1.0 + scalebuf[...]
    affine = project(
        jnp.concatenate([gain, shiftbuf[...], jnp.zeros((6, GW), F32)], axis=0), channels
    )
    early, late = backlog[:2], backlog[2:]
    absorb(early)
    for slot in late:
        sibling_arrived(slot[0])
    absorb(late)
    drain([("z", kv, half, part) for kv in ("k", "v") for part in (0, 1)])
    for part in (0, 1):
        some = pl.ds(part * NX // 2, NX // 2)
        for kv, buf in both:
            arrived(("z", kv, half, part))
            send(("s", kv, half, part), buf.at[half, 0, some], buf.at[half, 1, some], sibling)
    absorb([(half, 0)])
    for part in (0, 1):
        for kv in ("k", "v"):
            arrived(("s", kv, half, part))

    attended = []
    for h in range(GROUP_HEADS):
        _, totals, sums = absorbed(h, [(half, 1)])
        attended.append(sums / totals)
    mean = jnp.sum(sum(attended), axis=1, keepdims=True) / GW
    attended = [part - mean for part in attended]
    squares = jnp.sum(sum(part * part for part in attended), axis=1, keepdims=True)
    share = sum(
        project(attended[h] * gain[:, lanes_of(h)], channels[:, lanes_of(h)])
        for h in range(GROUP_HEADS)
    )
    lane = lax.rem(lax.broadcasted_iota(jnp.int32, share.shape, 1), SIDE)
    share = jnp.where(lane == width, mean, jnp.where(lane == width + 1, squares, share))
    slot = lax.broadcasted_iota(jnp.int32, (PACK, HEAD_DIM), 1) // STEP

    for side, d in [(1, 2), (1, 1), (1, 3), (0, 2), (0, 1), (0, 3), (1, 0), (0, 0)]:
        block = share[d * rows : (d + 1) * rows]
        strips = [
            block[:PACK],
            block[PACK : 2 * PACK],
            jnp.concatenate([block[2 * PACK :], affine], axis=0),
        ]
        strips = [turn(strip, i * STEP - side * SIDE) for i, strip in enumerate(strips)]
        packed = jnp.where(slot == 0, strips[0], jnp.where(slot == 1, strips[1], strips[2]))
        ysend[side, d] = packed
        if (side, d) == (0, 0):
            fetch("self", ysend.at[0, 0], yrecv.at[0, 0])
        else:
            if side:
                send(("other", d), ysend.at[1, d], yrecv.at[1, d], across(asker(d)))
            else:
                send(("own", d), ysend.at[0, d], yrecv.at[0, d], at(z, asker(d), core))

    drain()
    locals_["self"].wait()
    for d in NEAREST:
        arrived(("own", d))
    for d in range(NX):
        arrived(("other", d))


def combine(rows, width, yrecv, out_ref):
    def prediction(side):
        blocks = []
        for d in range(NX):
            packed = yrecv[side, d]
            blocks.append(
                jnp.concatenate([packed, turn(packed, -STEP), turn(packed, -2 * STEP)], axis=0)
            )
        means = [block[:rows, width : width + 1] for block in blocks]
        middle = sum(means) / NX
        spread_ = sum(block[:rows, width + 1 : width + 2] for block in blocks)
        spread_ = spread_ + GW * sum((mean_ - middle) * (mean_ - middle) for mean_ in means)
        inverse = lax.rsqrt(spread_ / (NX * GW) + EPSILON)
        linear = sum(
            block[:rows] + (mean_ - middle) * block[rows : rows + 1]
            for block, mean_ in zip(blocks, means)
        )
        return inverse * linear + sum(block[rows + 1 : rows + 2] for block in blocks)

    first = lax.axis_index("cfg") == 0
    own_weight = jnp.where(first, 1.0 - GUIDANCE, GUIDANCE)
    other_weight = jnp.where(first, GUIDANCE, 1.0 - GUIDANCE)
    guided = (own_weight * prediction(0) + other_weight * prediction(1)).T
    out_ref[0] = guided[:width]


def shards(nz, *args):
    (q, fk, fv, sk, sv, tk, tv, count, positions, shift, scale, proj) = args
    rows, features = q.shape[1], q.shape[2]
    words = tk.shape[1]
    width = proj.shape[1] // 2
    n_copies = len(copy_keys(nz))
    anywhere = pl.BlockSpec(memory_space=pl.ANY)
    in_vmem = pl.BlockSpec(memory_space=pltpu.VMEM)

    def body(*refs):
        kernel(nz, rows, *refs)

    returned = pl.pallas_call(
        body,
        out_shape=jax.ShapeDtypeStruct((2, NX, PACK, HEAD_DIM), F32),
        in_specs=[anywhere] * 12 + [pl.BlockSpec(memory_space=pltpu.SMEM)],
        out_specs=anywhere,
        scratch_shapes=[
            pltpu.VMEM((2, rows, features), BF16),
            pltpu.VMEM((NX - 1, rows, GW), BF16),
            pltpu.VMEM((NX - 1, rows, GW), BF16),
            pltpu.VMEM((NX, rows, GW), BF16),
            pltpu.VMEM((NX, rows, GW), BF16),
            pltpu.VMEM((NX, rows, GW), BF16),
            pltpu.VMEM((nz, NC, NX, rows, GW), BF16),
            pltpu.VMEM((nz, NC, NX, rows, GW), BF16),
            pltpu.VMEM((words, GW), BF16),
            pltpu.VMEM((words, GW), BF16),
            pltpu.VMEM((1, GW), F32),
            pltpu.VMEM((1, GW), F32),
            pltpu.VMEM((2 * width, GW), BF16),
            pltpu.VMEM((3, rows), jnp.int32),
            pltpu.VMEM((3, HEAD_DIM), F32),
            pltpu.VMEM((GROUP_HEADS, NX * rows, HEAD_DIM), BF16),
            pltpu.VMEM((GROUP_HEADS, NX * rows, HEAD_DIM), F32),
            pltpu.VMEM((GROUP_HEADS, NX * rows, HEAD_DIM), F32),
            pltpu.VMEM((GROUP_HEADS, NX * rows, HEAD_DIM), F32),
            pltpu.VMEM((2, NX, PACK, HEAD_DIM), F32),
            pltpu.SemaphoreType.DMA((13,)),
            pltpu.SemaphoreType.DMA((n_copies,)),
            pltpu.SemaphoreType.DMA((n_copies,)),
        ],
        compiler_params=pltpu.CompilerParams(
            collective_id=0, has_side_effects=True, vmem_limit_bytes=62 * 1024 * 1024
        ),
        name="stale_attention",
    )(
        q, fk, fv, sk, sv, tk, tv, shift, scale, proj.T, positions, jnp.asarray(lane_frequencies()), count
    )
    guided = pl.pallas_call(
        functools.partial(combine, rows, width),
        out_shape=jax.ShapeDtypeStruct((1, width, rows), F32),
        in_specs=[in_vmem],
        out_specs=in_vmem,
        name="guided_output",
    )(returned)
    return jnp.swapaxes(guided, 1, 2)


def solution(mesh):
    nz = mesh.shape["patch"] // (NX * NC)
    placed = (
        P("cfg", "patch", "rep"),
        P("cfg", "patch", "rep"),
        P("cfg", "patch", "rep"),
        P("cfg", "patch", "rep"),
        P("cfg", "patch", "rep"),
        P("cfg", "rep", None),
        P("cfg", "rep", None),
        P("cfg"),
        P("rep", "patch"),
        P("cfg", None),
        P("cfg", None),
        P(),
    )

    def run(*args):
        return shards(nz, *args)

    return jax.shard_map(
        run, mesh=mesh, in_specs=placed, out_specs=P("cfg", "patch", "rep"), check_vma=False
    )
```
